256 devices in a mesh: row: 16 (over z, core), col: 16 (over x, y).
Axes of the slice: x: 4, y: 4, z: 8, core: 2. Of those that a mesh axis runs over, the one named last changes fastest.
Arguments:
- object_tiles: float32 [2, 2048, 2048], P(None, 'row', 'col'), may hold values from -5 to 5
- probe: float32 [2, 128, 128], replicated, may hold values from -6 to 6
- amplitudes: float32 [4096, 128, 128], P(('row', 'col')), may hold values from 0 to 2.5
- offsets: int32 [4096, 2], P(('row', 'col')), may hold values from 0 to 128
- counts: int32 [16, 16], P('row', 'col'), may hold values from 1 to 16, as said below
- past_steps: float32 [4, 2, 2048, 2048], P(None, None, 'row', 'col'), may hold values from -32 to 32, as said below
- past_diffs: float32 [4, 2, 2048, 2048], P(None, None, 'row', 'col'), may hold values from -192 to 192
- last_gradient: float32 [2, 2048, 2048], P(None, 'row', 'col'), may hold values from -4 to 4
Outputs:
- object_grad: float32 [2, 2048, 2048], P(None, 'row', 'col')
- direction: float32 [2, 2048, 2048], P(None, 'row', 'col')
- probe_grad: float32 [2, 128, 128], replicated
- new_diff: float32 [2, 2048, 2048], P(None, 'row', 'col')
The draws below stay inside these ranges and needn't reach their ends.
Inputs may be any that keep to these rules, and one draw needn't show every extreme that they name: `counts`: slots of a tile from its count on are empty; some tile has all 16 slots live. past_steps[i] and past_diffs[i] have a positive inner product for every i.
All inputs are finite; a program needn't handle non-finite values.
Results may differ from the reference program's by a relative error of at most 0.0003.
Values sent between devices are 32-bit elements; how exact they have to be, the bound alone decides.
A program may use at most 64 MiB of HBM per device.

```python
import math
import jax
import jax.numpy as jnp
from jax import lax

PAT = 128
TILE = 128
P_DEV = 16
HIST = 4
NY = 2048
NX = 2048
SLOTS = 4096
N_ROW = 16
N_COL = 16


def history_base(key, spread):
    key_normal, key_scale = jax.random.split(key)
    pattern = jnp.clip(jax.random.normal(key_normal, (HIST, 2, NY, NX), jnp.float32), -4.0, 4.0)
    scales = jnp.exp(jax.random.uniform(key_scale, (HIST, 1, NY, 1), jnp.float32) * jnp.log(spread))
    return pattern * scales


def draw_counts(key, part):
    key = jax.random.fold_in(key, 3)
    key_spread, key_crowd, key_chosen = jax.random.split(key, 3)
    row_index = jnp.arange(N_ROW, dtype=jnp.int32)[:, None]
    floor_count = P_DEV // 8 + P_DEV // 4 * row_index // max(N_ROW - 1, 1)
    spread = jax.random.randint(key_spread, (N_ROW, N_COL), 0, P_DEV // 8 + 1)
    crowded = jax.random.randint(key_crowd, (N_ROW, N_COL), 0, 8) == 0
    filled = jnp.where(crowded, P_DEV, floor_count + spread).reshape(-1)
    chosen = jax.random.randint(key_chosen, (), 0, N_ROW * N_COL)
    filled = filled.at[chosen].set(P_DEV)
    return jnp.clip(filled, 1, P_DEV).reshape(N_ROW, N_COL).astype(jnp.int32)


def draw_past_steps(key, part):
    pattern = history_base(key, 2.0)
    return pattern


def draw_past_diffs(key, part):
    pattern = history_base(key, 2.0)
    key = jax.random.fold_in(key, 7)
    factor = jnp.exp(jax.random.uniform(key, (HIST, 2, NY, NX), jnp.float32, jnp.log(0.3), jnp.log(3.0)))
    return pattern * factor


def touch_ends(entries, own_key, least, high):
    longest = entries.shape.index(max(entries.shape))
    spots = []
    for shift in (0, 1):
        where = [jax.random.randint(jax.random.fold_in(own_key, axis), (), 0, length) for axis, length in enumerate(entries.shape)]
        where[longest] = (where[longest] + shift) % entries.shape[longest]
        spots.append(tuple(where))
    return entries.at[spots[0]].set(least).at[spots[1]].set(high)


def level_of(own_key, shape, cuts, smallest, high):
    def one(dim, blocks):
        draws = jax.random.uniform(jax.random.fold_in(jax.random.fold_in(own_key, 6), dim), (blocks,), jnp.float32, smallest / len(cuts), high / len(cuts))
        return jnp.repeat(jnp.exp(draws), shape[dim] // blocks).reshape((-1,) + (1,) * (len(shape) - dim - 1))

    level = one(*cuts[0])
    for cut in cuts[1:]:
        level = level * one(*cut)
    return level


def gaussian(stream_key, extent, scale, most, shards=(), held_as=jnp.bfloat16):
    drawn = scale * jax.random.normal(stream_key, extent, jnp.float32)
    if shards:
        drawn = drawn * level_of(stream_key, extent, shards, -0.22, 0.18)
    return jnp.clip(drawn, -most, most).astype(held_as)


def setup_inputs(seed: int = 0) -> dict:
    seeds = jax.random.split(jax.random.key(seed), 9)
    return {
        "object_tiles": gaussian(seeds[0], (2, NY, NX), 0.7, 5.0, ((1, 16), (2, 16)), jnp.float32),
        "probe": gaussian(seeds[1], (2, PAT, PAT), 1.0, 6.0, (), jnp.float32),
        "amplitudes": jnp.clip(2.5 * jax.random.uniform(seeds[2], (SLOTS, PAT, PAT), jnp.float32) ** level_of(seeds[2], (SLOTS, PAT, PAT), ((0, 256),), -0.2, 0.2), 0.0, 2.5),
        "offsets": touch_ends(jax.random.randint(seeds[3], (SLOTS, 2), 0, TILE + 1), jax.random.fold_in(seeds[3], 1), 0, TILE).astype(jnp.int32),
        "counts": draw_counts(jax.random.fold_in(seeds[8], 71), 0),
        "past_steps": draw_past_steps(jax.random.fold_in(seeds[8], 71), 0),
        "past_diffs": draw_past_diffs(jax.random.fold_in(seeds[8], 71), 0),
        "last_gradient": gaussian(seeds[7], (2, NY, NX), 0.3, 4.0, ((1, 16), (2, 16)), jnp.float32),
    }


precise = lax.Precision.HIGHEST
soften = 0.25

def tables(pattern_width):
    indices = jnp.arange(pattern_width, dtype=jnp.int32)
    product = indices[:, None] * indices[None, :] % pattern_width
    angle = product.astype(jnp.float32) * (2.0 * math.pi / pattern_width)
    factor = 1.0 / math.sqrt(pattern_width)
    return (jnp.cos(angle) * factor, jnp.sin(angle) * factor)

def from_left(matrix, field):
    return jnp.einsum('jk,bkl->bjl', matrix, field, precision=precise)

def from_right(field, matrix):
    return jnp.einsum('bjk,kl->bjl', field, matrix, precision=precise)

def transform(real_part, imag_part, cosine_table, sine_table, signum):
    left_real = from_left(cosine_table, real_part) + signum * from_left(sine_table, imag_part)
    left_imag = from_left(cosine_table, imag_part) - signum * from_left(sine_table, real_part)
    out_real = from_right(left_real, cosine_table) + signum * from_right(left_imag, sine_table)
    out_imag = from_right(left_imag, cosine_table) - signum * from_right(left_real, sine_table)
    return (out_real, out_imag)

def pattern_terms(patches, amplitudes, live, probe, cosine_table, sine_table):
    probe_real, probe_imag = (probe[0], probe[1])
    patch_real, patch_imag = (patches[:, 0], patches[:, 1])
    exit_real = probe_real * patch_real - probe_imag * patch_imag
    exit_imag = probe_real * patch_imag + probe_imag * patch_real
    far_real, far_imag = transform(exit_real, exit_imag, cosine_table, sine_table, 1.0)
    modulus = jnp.sqrt(far_real * far_real + far_imag * far_imag + soften)
    misfit = (modulus - amplitudes) * live[:, None, None]
    weight_real = 2.0 * misfit * far_real / modulus
    weight_imag = 2.0 * misfit * far_imag / modulus
    back_real, back_imag = transform(weight_real, weight_imag, cosine_table, sine_table, -1.0)
    object_real = probe_real * back_real + probe_imag * back_imag
    object_imag = probe_real * back_imag - probe_imag * back_real
    probe_term = jnp.stack([lax.optimization_barrier(jnp.sum(patch_real * back_real + patch_imag * back_imag, 0)), lax.optimization_barrier(jnp.sum(patch_real * back_imag - patch_imag * back_real, 0))])
    return (jnp.stack([object_real, object_imag], 1), probe_term)

def extract(padded, offsets, pattern_width):

    def cut(corner):
        return lax.dynamic_slice(padded, (jnp.int32(0), corner[0], corner[1]), (2, pattern_width, pattern_width))
    return jax.vmap(cut)(offsets)

def sweep_slots(patches, amplitudes, live_count, probe, cosine_table, sine_table):
    block_rows = min(8, patches.shape[0])

    def advance(i, carried):
        gradients, probe_total = carried
        first_slot = i * block_rows
        block_patch = lax.dynamic_slice_in_dim(patches, first_slot, block_rows, 0)
        block_amp = lax.dynamic_slice_in_dim(amplitudes, first_slot, block_rows, 0)
        live = (first_slot + jnp.arange(block_rows, dtype=jnp.int32) < live_count).astype(jnp.float32)
        block_grad, probe_term = pattern_terms(block_patch, block_amp, live, probe, cosine_table, sine_table)
        gradients = lax.dynamic_update_slice_in_dim(gradients, block_grad, first_slot, 0)
        return (gradients, probe_total + probe_term)
    block_count = (live_count + block_rows - 1) // block_rows
    initial = (jnp.zeros_like(patches), jnp.zeros(probe.shape, jnp.float32))
    return lax.fori_loop(jnp.int32(0), block_count, advance, initial)

def deposit(padded, gradients, offsets, live_count):
    pattern_width = gradients.shape[-1]

    def add_patch(k, field):
        corner = offsets[k]
        anchor = (jnp.int32(0), corner[0], corner[1])
        current = lax.dynamic_slice(field, anchor, (2, pattern_width, pattern_width))
        return lax.dynamic_update_slice(field, current + gradients[k], anchor)
    return lax.fori_loop(jnp.int32(0), live_count, add_patch, padded)

def two_loop(gradient, past_steps, past_diffs):
    history_len = past_steps.shape[0]
    inverse_curv = [1.0 / jnp.sum(past_steps[i] * past_diffs[i]) for i in range(history_len)]
    carried = gradient
    alphas = [None] * history_len
    for i in reversed(range(history_len)):
        alphas[i] = inverse_curv[i] * jnp.sum(past_steps[i] * carried)
        carried = carried - alphas[i] * past_diffs[i]
    scaling = jnp.sum(past_steps[-1] * past_diffs[-1]) / jnp.sum(past_diffs[-1] * past_diffs[-1])
    result = scaling * carried
    for i in range(history_len):
        correction = inverse_curv[i] * jnp.sum(past_diffs[i] * result)
        result = result + (alphas[i] - correction) * past_steps[i]
    return -result

def reference(object_tiles, probe, amplitudes, offsets, counts, past_steps, past_diffs, last_gradient):
    rim_width = PAT // 2
    obj_pad = jnp.pad(object_tiles, ((0, 0), (rim_width, rim_width), (rim_width, rim_width)))
    cosine_table, sine_table = tables(PAT)
    flat_counts = counts.reshape(-1)

    def per_tile(carried, tile_index):
        grad_pad, probe_total = carried
        tile_row = tile_index // N_COL
        tile_col = tile_index % N_COL
        tile_amp = lax.dynamic_slice_in_dim(amplitudes, tile_index * P_DEV, P_DEV, 0)
        tile_offsets = lax.dynamic_slice_in_dim(offsets, tile_index * P_DEV, P_DEV, 0)
        live_count = flat_counts[tile_index]
        anchor = jnp.stack([tile_row * TILE, tile_col * TILE]).astype(jnp.int32)
        shifted = tile_offsets + anchor[None, :]
        patches = extract(obj_pad, shifted, PAT)
        gradients, probe_term = sweep_slots(patches, tile_amp, live_count, probe, cosine_table, sine_table)
        grad_pad = deposit(grad_pad, gradients, shifted, live_count)
        return ((grad_pad, probe_total + probe_term), None)
    initial = (jnp.zeros(obj_pad.shape, jnp.float32), jnp.zeros(probe.shape, jnp.float32))
    tile_ids = jnp.arange(N_ROW * N_COL, dtype=jnp.int32)
    (grad_pad, probe_total), _ = lax.scan(per_tile, initial, tile_ids)
    total_live = jnp.sum(counts).astype(jnp.float32)
    object_grad = grad_pad[:, rim_width:rim_width + NY, rim_width:rim_width + NX] * (N_ROW * N_COL / total_live)
    probe_grad = probe_total / total_live
    direction = two_loop(object_grad, past_steps, past_diffs)
    new_diff = object_grad - last_gradient
    return (object_grad, direction, probe_grad, new_diff)
```

```python
import functools
import math

import jax
import jax.numpy as jnp
import numpy as np
from jax import lax
from jax.experimental import pallas as pl
from jax.experimental.pallas import tpu as pltpu
from jax.sharding import PartitionSpec as P

MESH = pl.DeviceIdType.MESH
F32 = jnp.float32
BF16 = jnp.bfloat16
W = 128
H = W // 2
SOFTEN = 0.25
GROUP = 4
HIST = 4

NORTH, SOUTH, WEST, EAST = (-1, 0), (1, 0), (0, -1), (0, 1)
NW, NE, SW, SE = (-1, -1), (-1, 1), (1, -1), (1, 1)
AROUND = (NORTH, SOUTH, WEST, EAST, NW, NE, SW, SE)
SIDES = AROUND[:4]
CORNERS = AROUND[4:]

PAIRS_SY = [(i, j) for i in range(HIST) for j in range(i, HIST)]
PAIRS_YY = [(i, j) for i in range(HIST) for j in range(i, HIST)]
ROW_SY = {pair: n for n, pair in enumerate(PAIRS_SY)}
ROW_YY = {pair: len(PAIRS_SY) + n for n, pair in enumerate(PAIRS_YY)}
ROW_COUNT = len(PAIRS_SY) + len(PAIRS_YY)
ROW_SG = ROW_COUNT + 1
ROW_YG = ROW_SG + HIST
N_DOTS = ROW_YG + HIST


def dft_tables():
    index = np.arange(W)
    angle = (index[:, None] * index[None, :] % W) * (2.0 * math.pi / W)
    cosine = np.cos(angle) / math.sqrt(W)
    sine = np.sin(angle) / math.sqrt(W)
    return np.stack([cosine, sine]).astype(np.float32)


def split(x):
    high = x.astype(BF16)
    return high, (x - high.astype(F32)).astype(BF16)


def mm(a, b):
    return jnp.dot(a, b, preferred_element_type=F32)


def kernel(
    n_row,
    n_col,
    slots,
    obj,
    probe,
    amp,
    off,
    cnt,
    steps,
    diffs,
    last,
    tabs,
    og_ref,
    dir_ref,
    pg_ref,
    nd_ref,
    pad,
    grad,
    pr_v,
    amp_v,
    s_v,
    y_v,
    last_v,
    trig,
    tab,
    patches,
    xh,
    xl,
    ah,
    al,
    zed,
    pacc,
    side_out,
    side_in,
    corner_out,
    corner_in,
    gside_in,
    gcorner_in,
    dots,
    rs_in,
    mix,
    row_in,
    mix2,
    col_in,
    loc_sem,
    halo_send,
    halo_recv,
    ghalo_send,
    ghalo_recv,
    rs_send,
    rs_recv,
    row_send,
    row_recv,
    col_send,
    col_recv,
):
    a = lax.axis_index("row")
    b = lax.axis_index("col")

    def at(step):
        return (lax.rem(a + step[0] % n_row, n_row), lax.rem(b + step[1] % n_col, n_col))

    def send(src, dst, send_sem, recv_sem, step):
        copy = pltpu.make_async_remote_copy(
            src_ref=src,
            dst_ref=dst,
            send_sem=send_sem,
            recv_sem=recv_sem,
            device_id=at(step),
            device_id_type=MESH,
        )
        copy.start()
        return copy

    def zero_at(index, edge):
        return jnp.where(index == edge, F32(0.0), F32(1.0))

    keep = {NORTH: zero_at(a, 0), SOUTH: zero_at(a, n_row - 1), WEST: zero_at(b, 0), EAST: zero_at(b, n_col - 1)}
    for dr, dc in CORNERS:
        keep[dr, dc] = keep[dr, 0] * keep[0, dc]

    obj_copy = pltpu.make_async_copy(obj, pad.at[0:2, H : H + W], loc_sem.at[0])
    obj_copy.start()
    local = []
    for n, (src, dst) in enumerate(
        ((steps, s_v), (diffs, y_v), (tabs, trig), (probe, pr_v), (amp, amp_v), (last, last_v))
    ):
        copy = pltpu.make_async_copy(src, dst, loc_sem.at[n + 1])
        copy.start()
        local.append(copy)

    partners = {(dr % n_row, dc % n_col) for dr, dc in AROUND}
    partners |= {(d, 0) for d in range(1, n_row)} | {(0, d) for d in range(1, n_col)}
    barrier = pltpu.get_barrier_semaphore()
    for step in sorted(partners):
        pl.semaphore_signal(barrier, inc=1, device_id=at(step), device_id_type=MESH)

    lane = lax.broadcasted_iota(jnp.int32, (H, W), 1)
    low = lane < H

    def turn(x):
        return pltpu.roll(x, H, 1)

    def pack(first, second):
        return jnp.where(low, first, second)

    obj_copy.wait()
    top = [pad[p, H : 2 * H] for p in range(2)]
    bottom = [pad[p, 2 * H : 3 * H] for p in range(2)]
    for p in range(2):
        side_out[0, p] = pack(top[p], turn(bottom[p]))
        side_out[1, p] = pack(turn(top[p]), bottom[p])
    for n, (dr, dc) in enumerate(CORNERS):
        rows = top if dr < 0 else bottom
        if dc < 0:
            corner_out[n] = pack(rows[0], turn(rows[1]))
        else:
            corner_out[n] = pack(turn(rows[0]), rows[1])

    pl.semaphore_wait(barrier, len(partners))

    def halo(north, south, north_dst, south_dst, sides, corners, send_sem, recv_sem):
        copies = []
        for n, step in enumerate(AROUND):
            if step == NORTH:
                src, dst = north, north_dst
            elif step == SOUTH:
                src, dst = south, south_dst
            elif n < 4:
                src, dst = side_out.at[n - 2], sides.at[n - 2]
            else:
                src, dst = corner_out.at[n - 4], corners.at[n - 4]
            copies.append(send(src, dst, send_sem.at[n], recv_sem.at[n], step))
        return copies

    halo_copies = halo(
        pad.at[0:2, H : 2 * H],
        pad.at[0:2, 2 * H : 3 * H],
        pad.at[0:2, 3 * H : 4 * H],
        pad.at[0:2, 0:H],
        side_in,
        corner_in,
        halo_send,
        halo_recv,
    )

    for copy in local[:2]:
        copy.wait()
    dots[...] = jnp.zeros_like(dots)
    flat = 2 * W

    def gram(n, sums):
        plane = n // (W // 8)
        rows = pl.ds(pl.multiple_of(lax.rem(n, W // 8) * 8, 8), 8)
        s = [s_v[i, plane, rows] for i in range(HIST)]
        y = [y_v[i, plane, rows] for i in range(HIST)]
        products = [s[i] * y[j] for i, j in PAIRS_SY] + [y[i] * y[j] for i, j in PAIRS_YY]
        return tuple(total + one for total, one in zip(sums, products))

    sums = lax.fori_loop(0, flat // 8, gram, (jnp.zeros((8, W), F32),) * ROW_COUNT)
    for n in range(ROW_COUNT):
        dots[n : n + 1] = jnp.sum(sums[n], 0, keepdims=True)
    live_count = cnt[0, 0]
    lane_row = lax.broadcasted_iota(jnp.int32, (1, W), 1)
    dots[ROW_COUNT : ROW_COUNT + 1] = jnp.where(lane_row == 0, live_count, 0).astype(F32)

    local[2].wait()
    parts = [split(trig[n]) for n in range(2)]
    for n in range(2):
        cosine, sine = parts[0][n], parts[1][n]
        for base, above, below in ((0, sine, -sine), (2, -sine, sine)):
            tab[base + n, 0:W, 0:W] = cosine
            tab[base + n, W:, W:] = cosine
            tab[base + n, 0:W, W:] = above
            tab[base + n, W:, 0:W] = below

    grad[...] = jnp.zeros_like(grad)
    pacc[...] = jnp.zeros_like(pacc)
    zed[...] = jnp.zeros_like(zed)

    for copy in halo_copies:
        copy.wait_recv()
    for copy in halo_copies:
        copy.wait_send()

    for p in range(2):
        pad[p, 0:H] = pad[p, 0:H] * keep[NORTH]
        pad[p, 3 * H : 4 * H] = pad[p, 3 * H : 4 * H] * keep[SOUTH]
        east = side_in[0, p] * keep[EAST]
        west = side_in[1, p] * keep[WEST]
        pad[2 + p, H : 2 * H] = pack(east, turn(west))
        pad[2 + p, 2 * H : 3 * H] = pack(turn(east), west)
    for rows, side in ((slice(0, H), -1), (slice(3 * H, 4 * H), 1)):
        from_east = corner_in[CORNERS.index((-side, -1))] * keep[side, 1]
        from_west = corner_in[CORNERS.index((-side, 1))] * keep[side, -1]
        pad[2, rows] = pack(from_east, turn(from_west))
        pad[3, rows] = pack(turn(from_east), from_west)

    for copy in local[3:5]:
        copy.wait()

    lanes = lax.broadcasted_iota(jnp.int32, (W, W), 1)
    lanes_h = lax.broadcasted_iota(jnp.int32, (H, W), 1)

    def own(q, iota):
        return (iota >= jnp.maximum(q, 0)) & (iota < jnp.minimum(q + W, W))

    def group(g, carry):
        first = g * GROUP
        offs = []
        for j in range(GROUP):
            k = first + j
            r, c = off[k, 0], off[k, 1]
            offs.append((r, c))
            inside = own(c - H, lanes)
            part = []
            for p in range(2):
                here = pad[p, pl.ds(r, W)]
                beside = pad[2 + p, pl.ds(r, W)]
                part.append(pltpu.roll(jnp.where(inside, here, beside), lax.rem(W + H - c, W), 1))
                patches[j, p] = part[p]
            pr, pi = pr_v[0], pr_v[1]
            cols = slice(j * W, (j + 1) * W)
            xh[0:W, cols], xl[0:W, cols] = split(pr * part[0] - pi * part[1])
            xh[W : 2 * W, cols], xl[W : 2 * W, cols] = split(pr * part[1] + pi * part[0])

        def left(high, low_part, emit):
            for h in range(GROUP // 2):
                cols = slice(h * 2 * W, (h + 1) * 2 * W)
                out = mm(high, xh[:, cols]) + mm(low_part, xh[:, cols]) + mm(high, xl[:, cols])
                for i in range(2):
                    emit(2 * h + i, out[0:W, i * W : (i + 1) * W], out[W:, i * W : (i + 1) * W])

        def right(high, low_part, emit):
            for h in range(GROUP // 2):
                rows = slice(h * 2 * W, (h + 1) * 2 * W)
                out = mm(ah[rows], high) + mm(ah[rows], low_part) + mm(al[rows], high)
                for i in range(2):
                    emit(2 * h + i, out[i * W : (i + 1) * W, 0:W], out[i * W : (i + 1) * W, W:])

        def to_rows(j, real, imag):
            rows = slice(j * W, (j + 1) * W)
            ah[rows, 0:W], al[rows, 0:W] = split(real)
            ah[rows, W:], al[rows, W:] = split(imag)

        def to_cols(j, real, imag):
            cols = slice(j * W, (j + 1) * W)
            xh[0:W, cols], xl[0:W, cols] = split(real)
            xh[W:, cols], xl[W:, cols] = split(imag)

        def weigh(j, real, imag):
            inverse = lax.rsqrt(real * real + imag * imag + SOFTEN)
            live = jnp.where(first + j < live_count, F32(2.0), F32(0.0))
            factor = live * (1.0 - amp_v[first + j] * inverse)
            to_rows(j, factor * real, factor * imag)

        def finish(j, real, imag):
            r, c = offs[j]
            pr, pi = pr_v[0], pr_v[1]
            shift = lax.rem(c + H, W)
            zed[j, 0, W : 2 * W] = pltpu.roll(pr * real + pi * imag, shift, 1)
            zed[j, 1, W : 2 * W] = pltpu.roll(pr * imag - pi * real, shift, 1)
            o_re, o_im = patches[j, 0], patches[j, 1]
            pacc[0:W] += o_re * real + o_im * imag
            pacc[W:] += o_re * imag - o_im * real

        left(tab[0], tab[1], to_rows)
        right(tab[2], tab[3], weigh)
        right(tab[0], tab[1], to_cols)
        left(tab[2], tab[3], finish)

        inside = [own(c - H, lanes_h) for _, c in offs]
        for ch in range(4):
            rows = slice(ch * H, (ch + 1) * H)
            for p in range(2):
                here, beside = grad[p, rows], grad[2 + p, rows]
                for j in range(GROUP):
                    moved = zed[j, p, pl.ds(W - offs[j][0] + ch * H, H)]
                    here += jnp.where(inside[j], moved, 0.0)
                    beside += jnp.where(inside[j], 0.0, moved)
                grad[p, rows], grad[2 + p, rows] = here, beside
        return carry

    lax.fori_loop(0, slots // GROUP, group, 0)

    for p in range(2):
        upper, lower = grad[2 + p, H : 2 * H], grad[2 + p, 2 * H : 3 * H]
        side_out[0, p] = pack(turn(upper), lower)
        side_out[1, p] = pack(upper, turn(lower))
    for n, (dr, dc) in enumerate(CORNERS):
        rows = slice(0, H) if dr < 0 else slice(3 * H, 4 * H)
        first, second = grad[2, rows], grad[3, rows]
        corner_out[n] = pack(turn(first), second) if dc < 0 else pack(first, turn(second))
    ghalo_copies = halo(
        grad.at[0:2, 0:H],
        grad.at[0:2, 3 * H : 4 * H],
        gside_in.at[2],
        gside_in.at[3],
        gside_in,
        gcorner_in,
        ghalo_send,
        ghalo_recv,
    )

    part = 2 * W // n_col
    rs_copies = []
    for d in range(1, n_col):
        rows = pl.ds(pl.multiple_of(lax.rem(b + d, n_col) * part, 8), part)
        rs_copies.append(send(pacc.at[rows], rs_in.at[d - 1], rs_send.at[d - 1], rs_recv.at[d - 1], (0, d)))

    for copy in ghalo_copies:
        copy.wait_recv()
    for p in range(2):
        east, west = gside_in[0, p] * keep[EAST], gside_in[1, p] * keep[WEST]
        for side, mid in ((-1, pack(west, turn(east))), (1, pack(turn(west), east))):
            from_east = gcorner_in[CORNERS.index((-side, -1))] * keep[side, 1]
            from_west = gcorner_in[CORNERS.index((-side, 1))] * keep[side, -1]
            if p == 0:
                corner = pack(from_west, turn(from_east))
            else:
                corner = pack(turn(from_west), from_east)
            vertical = gside_in[3 if side < 0 else 2, p] * keep[side, 0]
            mine = grad[p, H : 2 * H] if side < 0 else grad[p, 2 * H : 3 * H]
            if side < 0:
                og_ref[p, 0:H] = mine + vertical + mid + corner
            else:
                og_ref[p, H:] = mine + vertical + mid + corner

    def with_gradient(n, sums):
        plane = n // (W // 8)
        rows = pl.ds(pl.multiple_of(lax.rem(n, W // 8) * 8, 8), 8)
        g = og_ref[plane, rows]
        products = [s_v[i, plane, rows] * g for i in range(HIST)] + [y_v[i, plane, rows] * g for i in range(HIST)]
        return tuple(total + one for total, one in zip(sums, products))

    sums = lax.fori_loop(0, flat // 8, with_gradient, (jnp.zeros((8, W), F32),) * (2 * HIST))
    for n in range(2 * HIST):
        dots[ROW_SG + n : ROW_SG + n + 1] = jnp.sum(sums[n], 0, keepdims=True)
    ones = jnp.ones((8, W), F32)
    mix[0:8] = lax.dot_general(
        ones, dots[...], (((1,), (1,)), ((), ())), precision=lax.Precision.HIGHEST, preferred_element_type=F32
    )

    for copy in rs_copies:
        copy.wait_recv()
    total = pacc[pl.ds(pl.multiple_of(b * part, 8), part)]
    for d in range(n_col - 1):
        total += rs_in[d]
    mix[8:] = total

    row_copies = [
        send(mix, row_in.at[d - 1], row_send.at[d - 1], row_recv.at[d - 1], (d, 0)) for d in range(1, n_row)
    ]
    for copy in row_copies:
        copy.wait_recv()
    total = mix[...]
    for d in range(n_row - 1):
        total += row_in[d]
    mix2[...] = total

    col_copies = [
        send(mix2, col_in.at[d - 1], col_send.at[d - 1], col_recv.at[d - 1], (0, d)) for d in range(1, n_col)
    ]
    local[5].wait()
    for copy in col_copies:
        copy.wait_recv()
    total = mix2[0:8]
    for d in range(n_col - 1):
        total += col_in[d, 0:8]

    value = [jnp.broadcast_to(total[:, n : n + 1], (8, W)) for n in range(N_DOTS)]
    live_total = value[ROW_COUNT]
    per_live = 1.0 / live_total
    scale = (n_row * n_col) * per_live
    sg = [value[ROW_SG + i] * scale for i in range(HIST)]
    yg = [value[ROW_YG + i] * scale for i in range(HIST)]
    rho = [1.0 / value[ROW_SY[i, i]] for i in range(HIST)]
    alpha = [None] * HIST
    for i in reversed(range(HIST)):
        inner = sg[i]
        for j in range(i + 1, HIST):
            inner = inner - alpha[j] * value[ROW_SY[i, j]]
        alpha[i] = rho[i] * inner
    gamma = value[ROW_SY[HIST - 1, HIST - 1]] / value[ROW_YY[HIST - 1, HIST - 1]]
    weight = [None] * HIST
    for i in range(HIST):
        inner = yg[i]
        for j in range(HIST):
            inner = inner - alpha[j] * value[ROW_YY[min(i, j), max(i, j)]]
        inner = gamma * inner
        for j in range(i):
            inner = inner + weight[j] * value[ROW_SY[j, i]]
        weight[i] = alpha[i] - rho[i] * inner

    def wide(x, rows):
        return jnp.broadcast_to(x[0:1], (rows, W))

    def finish_rows(n, carry):
        plane = n // (W // 8)
        rows = pl.ds(pl.multiple_of(lax.rem(n, W // 8) * 8, 8), 8)
        g = og_ref[plane, rows] * scale
        og_ref[plane, rows] = g
        nd_ref[plane, rows] = g - last_v[plane, rows]
        q = g
        for i in range(HIST):
            q = q - alpha[i] * y_v[i, plane, rows]
        q = gamma * q
        for i in range(HIST):
            q = q + weight[i] * s_v[i, plane, rows]
        dir_ref[plane, rows] = -q
        return carry

    lax.fori_loop(0, flat // 8, finish_rows, 0)

    pg_ref[pl.ds(pl.multiple_of(b * part, 8), part)] = mix2[8:] * wide(per_live, part)
    for d in range(1, n_col):
        rows = pl.ds(pl.multiple_of(lax.rem(b + n_col - d, n_col) * part, 8), part)
        pg_ref[rows] = col_in[d - 1, 8:] * wide(per_live, part)

    for copy in ghalo_copies + rs_copies + row_copies + col_copies:
        copy.wait_send()


def store(a, b, c, d, a_out, b_out, c_out, d_out, sem):
    copies = [
        pltpu.make_async_copy(src, dst, sem.at[n])
        for n, (src, dst) in enumerate(((a, a_out), (b, b_out), (c, c_out), (d, d_out)))
    ]
    for copy in copies:
        copy.start()
    for copy in copies:
        copy.wait()


def body(n_row, n_col, object_tiles, probe, amplitudes, offsets, counts, past_steps, past_diffs, last_gradient):
    slots = amplitudes.shape[0]
    part = 2 * W // n_col
    plane_pair = jax.ShapeDtypeStruct((2, W, W), F32)
    any_spec = pl.BlockSpec(memory_space=pltpu.HBM)
    smem_spec = pl.BlockSpec(memory_space=pltpu.SMEM)
    vmem_spec = pl.BlockSpec(memory_space=pltpu.VMEM)
    dma = pltpu.SemaphoreType.DMA
    scratch = [
        pltpu.VMEM((4, 4 * H, W), F32),
        pltpu.VMEM((4, 4 * H, W), F32),
        pltpu.VMEM((2, W, W), F32),
        pltpu.VMEM((slots, W, W), F32),
        pltpu.VMEM((HIST, 2, W, W), F32),
        pltpu.VMEM((HIST, 2, W, W), F32),
        pltpu.VMEM((2, W, W), F32),
        pltpu.VMEM((2, W, W), F32),
        pltpu.VMEM((4, 2 * W, 2 * W), BF16),
        pltpu.VMEM((GROUP, 2, W, W), F32),
        pltpu.VMEM((2 * W, GROUP * W), BF16),
        pltpu.VMEM((2 * W, GROUP * W), BF16),
        pltpu.VMEM((GROUP * W, 2 * W), BF16),
        pltpu.VMEM((GROUP * W, 2 * W), BF16),
        pltpu.VMEM((GROUP, 2, 3 * W, W), F32),
        pltpu.VMEM((2 * W, W), F32),
        pltpu.VMEM((2, 2, H, W), F32),
        pltpu.VMEM((2, 2, H, W), F32),
        pltpu.VMEM((4, H, W), F32),
        pltpu.VMEM((4, H, W), F32),
        pltpu.VMEM((4, 2, H, W), F32),
        pltpu.VMEM((4, H, W), F32),
        pltpu.VMEM((W, W), F32),
        pltpu.VMEM((n_col - 1, part, W), F32),
        pltpu.VMEM((8 + part, W), F32),
        pltpu.VMEM((n_row - 1, 8 + part, W), F32),
        pltpu.VMEM((8 + part, W), F32),
        pltpu.VMEM((n_col - 1, 8 + part, W), F32),
        dma((7,)),
        dma((8,)),
        dma((8,)),
        dma((8,)),
        dma((8,)),
        dma((n_col - 1,)),
        dma((n_col - 1,)),
        dma((n_row - 1,)),
        dma((n_row - 1,)),
        dma((n_col - 1,)),
        dma((n_col - 1,)),
    ]
    og, direction, pg, nd = pl.pallas_call(
        functools.partial(kernel, n_row, n_col, slots),
        name="ptycho",
        out_shape=(plane_pair, plane_pair, jax.ShapeDtypeStruct((2 * W, W), F32), plane_pair),
        in_specs=[any_spec, any_spec, any_spec, smem_spec, smem_spec, any_spec, any_spec, any_spec, any_spec],
        out_specs=(vmem_spec,) * 4,
        scratch_shapes=scratch,
        compiler_params=pltpu.CompilerParams(
            collective_id=0, has_side_effects=True, vmem_limit_bytes=62 * 2**20
        ),
    )(
        object_tiles,
        probe,
        amplitudes,
        offsets,
        counts,
        past_steps,
        past_diffs,
        last_gradient,
        jnp.asarray(dft_tables()),
    )
    return pl.pallas_call(
        store,
        name="store",
        out_shape=(plane_pair,) * 4,
        in_specs=[vmem_spec] * 4,
        out_specs=(any_spec,) * 4,
        scratch_shapes=[dma((4,))],
    )(og, direction, pg.reshape(2, W, W), nd)


def solution(mesh):
    return jax.shard_map(
        functools.partial(body, mesh.shape["row"], mesh.shape["col"]),
        mesh=mesh,
        in_specs=(
            P(None, "row", "col"),
            P(),
            P(("row", "col"), None, None),
            P(("row", "col"), None),
            P("row", "col"),
            P(None, None, "row", "col"),
            P(None, None, "row", "col"),
            P(None, "row", "col"),
        ),
        out_specs=(P(None, "row", "col"), P(None, "row", "col"), P(), P(None, "row", "col")),
        check_vma=False,
    )
```

```python
import functools
import math

import jax
import jax.numpy as jnp
import numpy as np
from jax import lax
from jax.experimental import pallas as pl
from jax.experimental.pallas import tpu as pltpu
from jax.sharding import PartitionSpec as P

MESH = pl.DeviceIdType.MESH
F32 = jnp.float32
BF16 = jnp.bfloat16
W = 128
H = W // 2
SOFTEN = 0.25
GROUP = 4
HIST = 4

NORTH, SOUTH, WEST, EAST = (-1, 0), (1, 0), (0, -1), (0, 1)
NW, NE, SW, SE = (-1, -1), (-1, 1), (1, -1), (1, 1)
AROUND = (NORTH, SOUTH, WEST, EAST, NW, NE, SW, SE)
SIDES = AROUND[:4]
CORNERS = AROUND[4:]

PAIRS_SY = [(i, j) for i in range(HIST) for j in range(i, HIST)]
PAIRS_YY = [(i, j) for i in range(HIST) for j in range(i, HIST)]
ROW_SY = {pair: n for n, pair in enumerate(PAIRS_SY)}
ROW_YY = {pair: len(PAIRS_SY) + n for n, pair in enumerate(PAIRS_YY)}
ROW_COUNT = len(PAIRS_SY) + len(PAIRS_YY)
ROW_SG = ROW_COUNT + 1
ROW_YG = ROW_SG + HIST
N_DOTS = ROW_YG + HIST


def dft_tables():
    index = np.arange(W)
    angle = (index[:, None] * index[None, :] % W) * (2.0 * math.pi / W)
    cosine = np.cos(angle) / math.sqrt(W)
    sine = np.sin(angle) / math.sqrt(W)
    return np.stack([cosine, sine]).astype(np.float32)


def split(x):
    high = x.astype(BF16)
    return high, (x - high.astype(F32)).astype(BF16)


def mm(a, b):
    return jnp.dot(a, b, preferred_element_type=F32)


def kernel(
    n_row,
    n_col,
    slots,
    obj,
    probe,
    amp,
    off,
    cnt,
    steps,
    diffs,
    last,
    tabs,
    og_ref,
    dir_ref,
    pg_ref,
    nd_ref,
    pad,
    grad,
    pr_v,
    amp_v,
    s_v,
    y_v,
    last_v,
    trig,
    tab,
    patches,
    xh,
    xl,
    ah,
    al,
    zed,
    pacc,
    side_out,
    side_in,
    corner_out,
    corner_in,
    gside_in,
    gcorner_in,
    dots,
    half_in,
    rs_in,
    mix,
    row_in,
    mix2,
    col_in,
    loc_sem,
    halo_send,
    halo_recv,
    ghalo_send,
    ghalo_recv,
    sum_send,
    sum_recv,
):
    a = lax.axis_index("row")
    b = lax.axis_index("col")

    def at(step):
        return (lax.rem(a + step[0] % n_row, n_row), lax.rem(b + step[1] % n_col, n_col))

    def send(src, dst, send_sem, recv_sem, device):
        pltpu.make_async_remote_copy(
            src_ref=src,
            dst_ref=dst,
            send_sem=send_sem,
            recv_sem=recv_sem,
            device_id=device,
            device_id_type=MESH,
        ).start()

    def zero_at(index, edge):
        return jnp.where(index == edge, F32(0.0), F32(1.0))

    keep = {NORTH: zero_at(a, 0), SOUTH: zero_at(a, n_row - 1), WEST: zero_at(b, 0), EAST: zero_at(b, n_col - 1)}
    for dr, dc in CORNERS:
        keep[dr, dc] = keep[dr, 0] * keep[0, dc]

    core = lax.rem(a, 2)
    mate = (a + 1 - 2 * core, b)
    obj_copy = pltpu.make_async_copy(obj, pad.at[0:2, H : H + W], loc_sem.at[0])
    obj_copy.start()
    partners = [(dr % n_row, dc % n_col) for dr, dc in AROUND]
    others = [(d, 0) for d in range(1, n_row)] + [(0, d) for d in range(1, n_col)]
    partners += [step for step in others if step not in partners]
    barrier = pltpu.get_barrier_semaphore()
    for step in partners:
        pl.semaphore_signal(barrier, inc=1, device_id=at(step), device_id_type=MESH)
    local = []
    for n, (src, dst) in enumerate(
        ((steps, s_v), (diffs, y_v), (tabs, trig), (probe, pr_v), (amp, amp_v), (last, last_v))
    ):
        copy = pltpu.make_async_copy(src, dst, loc_sem.at[n + 1])
        copy.start()
        local.append(copy)

    def drain(ref, sem):
        pltpu.make_async_copy(ref, ref, sem).wait()

    lane = lax.broadcasted_iota(jnp.int32, (H, W), 1)
    low = lane < H

    def turn(x):
        return pltpu.roll(x, H, 1)

    def pack(first, second):
        return jnp.where(low, first, second)

    obj_copy.wait()
    top = [pad[p, H : 2 * H] for p in range(2)]
    bottom = [pad[p, 2 * H : 3 * H] for p in range(2)]
    for p in range(2):
        side_out[0, p] = pack(top[p], turn(bottom[p]))
        side_out[1, p] = pack(turn(top[p]), bottom[p])
    for n, (dr, dc) in enumerate(CORNERS):
        rows = top if dr < 0 else bottom
        if dc < 0:
            corner_out[n] = pack(rows[0], turn(rows[1]))
        else:
            corner_out[n] = pack(turn(rows[0]), rows[1])

    pl.semaphore_wait(barrier, len(partners))

    for n, step in enumerate(CORNERS):
        send(corner_out.at[n], corner_in.at[n], halo_send.at[1], halo_recv.at[1], at(step))
    for n, step in enumerate((WEST, EAST)):
        send(side_out.at[n], side_in.at[n], halo_send.at[0], halo_recv.at[0], at(step))
    first_rows, last_rows = pad.at[0:2, 0:H], pad.at[0:2, 3 * H : 4 * H]
    send(pad.at[0:2, H : 2 * H], last_rows, halo_send.at[2], halo_recv.at[2], at(NORTH))
    send(pad.at[0:2, 2 * H : 3 * H], first_rows, halo_send.at[3], halo_recv.at[3], at(SOUTH))

    for copy in local[:2]:
        copy.wait()
    dots[...] = jnp.zeros_like(dots)
    flat = 2 * W

    def gram(n, sums):
        plane = n // (W // 8)
        rows = pl.ds(pl.multiple_of(lax.rem(n, W // 8) * 8, 8), 8)
        s = [s_v[i, plane, rows] for i in range(HIST)]
        y = [y_v[i, plane, rows] for i in range(HIST)]
        products = [s[i] * y[j] for i, j in PAIRS_SY] + [y[i] * y[j] for i, j in PAIRS_YY]
        return tuple(total + one for total, one in zip(sums, products))

    sums = lax.fori_loop(0, flat // 8, gram, (jnp.zeros((8, W), F32),) * ROW_COUNT)
    for n in range(ROW_COUNT):
        dots[n : n + 1] = jnp.sum(sums[n], 0, keepdims=True)
    live_count = cnt[0, 0]
    lane_row = lax.broadcasted_iota(jnp.int32, (1, W), 1)
    dots[ROW_COUNT : ROW_COUNT + 1] = jnp.where(lane_row == 0, live_count, 0).astype(F32)
    mix[0:8] = lax.dot_general(
        jnp.ones((8, W), F32),
        dots[...],
        (((1,), (1,)), ((), ())),
        precision=lax.Precision.HIGHEST,
        preferred_element_type=F32,
    )

    local[2].wait()
    parts = [split(trig[n]) for n in range(2)]
    for n in range(2):
        cosine, sine = parts[0][n], parts[1][n]
        for base, above, below in ((0, sine, -sine), (2, -sine, sine)):
            tab[base + n, 0:W, 0:W] = cosine
            tab[base + n, W:, W:] = cosine
            tab[base + n, 0:W, W:] = above
            tab[base + n, W:, 0:W] = below

    grad[...] = jnp.zeros_like(grad)
    pacc[...] = jnp.zeros_like(pacc)
    zed[...] = jnp.zeros_like(zed)

    for copy in local[3:5]:
        copy.wait()
    for sems in (halo_send, halo_recv):
        for n, ref in enumerate((side_in, corner_in, last_rows, first_rows)):
            drain(ref, sems.at[n])

    for p in range(2):
        pad[p, 0:H] = pad[p, 0:H] * keep[NORTH]
        pad[p, 3 * H : 4 * H] = pad[p, 3 * H : 4 * H] * keep[SOUTH]
        east = side_in[0, p] * keep[EAST]
        west = side_in[1, p] * keep[WEST]
        pad[2 + p, H : 2 * H] = pack(east, turn(west))
        pad[2 + p, 2 * H : 3 * H] = pack(turn(east), west)
    for rows, side in ((slice(0, H), -1), (slice(3 * H, 4 * H), 1)):
        from_east = corner_in[CORNERS.index((-side, -1))] * keep[side, 1]
        from_west = corner_in[CORNERS.index((-side, 1))] * keep[side, -1]
        pad[2, rows] = pack(from_east, turn(from_west))
        pad[3, rows] = pack(turn(from_east), from_west)

    lanes = lax.broadcasted_iota(jnp.int32, (W, W), 1)
    lanes_h = lax.broadcasted_iota(jnp.int32, (H, W), 1)

    def own(q, iota):
        return (iota >= jnp.maximum(q, 0)) & (iota < jnp.minimum(q + W, W))

    def group(g, carry):
        first = g * GROUP
        offs = []
        for j in range(GROUP):
            k = first + j
            r, c = off[0, k], off[1, k]
            offs.append((r, c))
            inside = own(c - H, lanes)
            part = []
            for p in range(2):
                here = pad[p, pl.ds(r, W)]
                beside = pad[2 + p, pl.ds(r, W)]
                part.append(pltpu.roll(jnp.where(inside, here, beside), lax.rem(W + H - c, W), 1))
                patches[j, p] = part[p]
            pr, pi = pr_v[0], pr_v[1]
            cols = slice(j * W, (j + 1) * W)
            xh[0:W, cols], xl[0:W, cols] = split(pr * part[0] - pi * part[1])
            xh[W : 2 * W, cols], xl[W : 2 * W, cols] = split(pr * part[1] + pi * part[0])

        def left(high, low_part, emit):
            for h in range(GROUP // 2):
                cols = slice(h * 2 * W, (h + 1) * 2 * W)
                out = mm(high, xh[:, cols]) + mm(low_part, xh[:, cols]) + mm(high, xl[:, cols])
                for i in range(2):
                    emit(2 * h + i, out[0:W, i * W : (i + 1) * W], out[W:, i * W : (i + 1) * W])

        def right(high, low_part, emit):
            for h in range(GROUP // 2):
                rows = slice(h * 2 * W, (h + 1) * 2 * W)
                out = mm(ah[rows], high) + mm(ah[rows], low_part) + mm(al[rows], high)
                for i in range(2):
                    emit(2 * h + i, out[i * W : (i + 1) * W, 0:W], out[i * W : (i + 1) * W, W:])

        def to_rows(j, real, imag):
            rows = slice(j * W, (j + 1) * W)
            ah[rows, 0:W], al[rows, 0:W] = split(real)
            ah[rows, W:], al[rows, W:] = split(imag)

        def to_cols(j, real, imag):
            cols = slice(j * W, (j + 1) * W)
            xh[0:W, cols], xl[0:W, cols] = split(real)
            xh[W:, cols], xl[W:, cols] = split(imag)

        def weigh(j, real, imag):
            inverse = lax.rsqrt(real * real + imag * imag + SOFTEN)
            live = jnp.where(first + j < live_count, F32(2.0), F32(0.0))
            factor = live * (1.0 - amp_v[first + j] * inverse)
            to_rows(j, factor * real, factor * imag)

        def finish(j, real, imag):
            r, c = offs[j]
            pr, pi = pr_v[0], pr_v[1]
            shift = lax.rem(c + H, W)
            zed[j, 0, W : 2 * W] = pltpu.roll(pr * real + pi * imag, shift, 1)
            zed[j, 1, W : 2 * W] = pltpu.roll(pr * imag - pi * real, shift, 1)
            o_re, o_im = patches[j, 0], patches[j, 1]
            pacc[0:W] += o_re * real + o_im * imag
            pacc[W:] += o_re * imag - o_im * real

        left(tab[0], tab[1], to_rows)
        right(tab[2], tab[3], weigh)
        right(tab[0], tab[1], to_cols)
        left(tab[2], tab[3], finish)

        inside = [own(c - H, lanes_h) for _, c in offs]
        for ch in range(4):
            rows = slice(ch * H, (ch + 1) * H)
            for p in range(2):
                here, beside = grad[p, rows], grad[2 + p, rows]
                for j in range(GROUP):
                    moved = zed[j, p, pl.ds(W - offs[j][0] + ch * H, H)]
                    here += jnp.where(inside[j], moved, 0.0)
                    beside += jnp.where(inside[j], 0.0, moved)
                grad[p, rows], grad[2 + p, rows] = here, beside
        return carry

    lax.fori_loop(0, slots // GROUP, group, 0)

    other_plane = pl.ds(pl.multiple_of((1 - core) * W, W), W)
    send(pacc.at[other_plane], half_in, sum_send.at[0], sum_recv.at[0], mate)

    for p in range(2):
        upper, lower = grad[2 + p, H : 2 * H], grad[2 + p, 2 * H : 3 * H]
        side_out[0, p] = pack(turn(upper), lower)
        side_out[1, p] = pack(upper, turn(lower))
    for n, (dr, dc) in enumerate(CORNERS):
        rows = slice(0, H) if dr < 0 else slice(3 * H, 4 * H)
        first, second = grad[2, rows], grad[3, rows]
        corner_out[n] = pack(turn(first), second) if dc < 0 else pack(first, turn(second))
    for n, step in enumerate(CORNERS):
        send(corner_out.at[n], gcorner_in.at[n], ghalo_send.at[1], ghalo_recv.at[1], at(step))
    for n, (src, step) in enumerate(
        (
            (side_out.at[0], WEST),
            (side_out.at[1], EAST),
            (grad.at[0:2, 0:H], NORTH),
            (grad.at[0:2, 3 * H : 4 * H], SOUTH),
        )
    ):
        send(src, gside_in.at[n], ghalo_send.at[0], ghalo_recv.at[0], at(step))

    part = W // n_col

    def plane_rows(plane, start, size):
        return pl.ds(pl.multiple_of(plane * W + start, 8), size)

    drain(half_in, sum_recv.at[0])
    pacc[plane_rows(core, 0, W)] += half_in[...]
    for d in range(1, n_col):
        rows = plane_rows(core, lax.rem(b + d, n_col) * part, part)
        send(pacc.at[rows], rs_in.at[d - 1], sum_send.at[1], sum_recv.at[1], at((0, d)))

    drain(gside_in, ghalo_recv.at[0])
    drain(gcorner_in, ghalo_recv.at[1])
    for p in range(2):
        east, west = gside_in[0, p] * keep[EAST], gside_in[1, p] * keep[WEST]
        for side, mid in ((-1, pack(west, turn(east))), (1, pack(turn(west), east))):
            from_east = gcorner_in[CORNERS.index((-side, -1))] * keep[side, 1]
            from_west = gcorner_in[CORNERS.index((-side, 1))] * keep[side, -1]
            if p == 0:
                corner = pack(from_west, turn(from_east))
            else:
                corner = pack(turn(from_west), from_east)
            vertical = gside_in[3 if side < 0 else 2, p] * keep[side, 0]
            mine = grad[p, H : 2 * H] if side < 0 else grad[p, 2 * H : 3 * H]
            if side < 0:
                og_ref[p, 0:H] = mine + vertical + mid + corner
            else:
                og_ref[p, H:] = mine + vertical + mid + corner

    def with_gradient(n, sums):
        plane = n // (W // 8)
        rows = pl.ds(pl.multiple_of(lax.rem(n, W // 8) * 8, 8), 8)
        g = og_ref[plane, rows]
        products = [s_v[i, plane, rows] * g for i in range(HIST)] + [y_v[i, plane, rows] * g for i in range(HIST)]
        return tuple(total + one for total, one in zip(sums, products))

    sums = lax.fori_loop(0, flat // 8, with_gradient, (jnp.zeros((8, W), F32),) * (2 * HIST))
    row8 = lax.broadcasted_iota(jnp.int32, (8, W), 0)
    lane8 = lax.broadcasted_iota(jnp.int32, (8, W), 1)
    inner = jnp.zeros((8, W), F32)
    for n in range(2 * HIST):
        inner = jnp.where(row8 == n, jnp.sum(sums[n], 0, keepdims=True), inner)
    inner = jnp.sum(inner, 1, keepdims=True)
    mix[0:8] = jnp.where(lane8 == ROW_SG + row8, inner, jnp.where(row8 == 0, mix[0:8], 0.0))

    drain(rs_in, sum_recv.at[1])
    total = pacc[plane_rows(core, b * part, part)]
    for d in range(n_col - 1):
        total += rs_in[d]
    mix[8:] = total

    for d in range(1, n_row):
        send(mix, row_in.at[d - 1], sum_send.at[2], sum_recv.at[2], at((d, 0)))
    drain(half_in, sum_send.at[0])
    drain(rs_in, sum_send.at[1])
    drain(gside_in, ghalo_send.at[0])
    drain(gcorner_in, ghalo_send.at[1])
    drain(row_in, sum_recv.at[2])
    own, odd = mix[...], row_in[0]
    for d in range(2, n_row):
        if d % 2 == 0:
            own += row_in[d - 1]
        else:
            odd += row_in[d - 1]
    mix2[0:8] = own[0:8] + odd[0:8]
    mix2[8 : 8 + part] = own[8:]
    mix2[8 + part :] = odd[8:]

    for d in range(1, n_col):
        send(mix2, col_in.at[d - 1], sum_send.at[3], sum_recv.at[3], at((0, d)))
    drain(row_in, sum_send.at[2])
    local[5].wait()
    drain(col_in, sum_recv.at[3])
    total = mix2[0:8]
    for d in range(n_col - 1):
        total += col_in[d, 0:8]
    total = jnp.broadcast_to(jnp.sum(total, 0, keepdims=True), (8, W))

    value = [jnp.broadcast_to(total[:, n : n + 1], (8, W)) for n in range(N_DOTS)]
    live_total = value[ROW_COUNT]
    per_live = 1.0 / live_total
    scale = (n_row * n_col) * per_live
    sg = [value[ROW_SG + i] * scale for i in range(HIST)]
    yg = [value[ROW_YG + i] * scale for i in range(HIST)]
    rho = [1.0 / value[ROW_SY[i, i]] for i in range(HIST)]
    alpha = [None] * HIST
    for i in reversed(range(HIST)):
        inner = sg[i]
        for j in range(i + 1, HIST):
            inner = inner - alpha[j] * value[ROW_SY[i, j]]
        alpha[i] = rho[i] * inner
    gamma = value[ROW_SY[HIST - 1, HIST - 1]] / value[ROW_YY[HIST - 1, HIST - 1]]
    weight = [None] * HIST
    for i in range(HIST):
        inner = yg[i]
        for j in range(HIST):
            inner = inner - alpha[j] * value[ROW_YY[min(i, j), max(i, j)]]
        inner = gamma * inner
        for j in range(i):
            inner = inner + weight[j] * value[ROW_SY[j, i]]
        weight[i] = alpha[i] - rho[i] * inner

    def finish_rows(n, carry):
        plane = n // (W // 8)
        rows = pl.ds(pl.multiple_of(lax.rem(n, W // 8) * 8, 8), 8)
        g = og_ref[plane, rows] * scale
        og_ref[plane, rows] = g
        nd_ref[plane, rows] = g - last_v[plane, rows]
        q = g
        for i in range(HIST):
            q = q - alpha[i] * y_v[i, plane, rows]
        q = gamma * q
        for i in range(HIST):
            q = q + weight[i] * s_v[i, plane, rows]
        dir_ref[plane, rows] = -q
        return carry

    lax.fori_loop(0, flat // 8, finish_rows, 0)

    weight_live = per_live[0:part]
    for d in range(n_col):
        col = lax.rem(b + n_col - d, n_col) * part
        found = mix2 if d == 0 else col_in.at[d - 1]
        pg_ref[plane_rows(core, col, part)] = found[8 : 8 + part] * weight_live
        pg_ref[plane_rows(1 - core, col, part)] = found[8 + part :] * weight_live
    drain(col_in, sum_send.at[3])


def store(a, b, c, d, a_out, b_out, c_out, d_out, sem):
    copies = [
        pltpu.make_async_copy(src, dst, sem.at[n])
        for n, (src, dst) in enumerate(((a, a_out), (b, b_out), (c, c_out), (d, d_out)))
    ]
    for copy in copies:
        copy.start()
    for copy in copies:
        copy.wait()


def body(n_row, n_col, object_tiles, probe, amplitudes, offsets, counts, past_steps, past_diffs, last_gradient):
    slots = amplitudes.shape[0]
    part = W // n_col
    object_tiles, probe, amplitudes, offsets, past_steps, past_diffs, last_gradient, tables = [
        pltpu.with_memory_space_constraint(x, pltpu.HBM)
        for x in (
            object_tiles,
            probe,
            amplitudes,
            offsets.T,
            past_steps,
            past_diffs,
            last_gradient,
            jnp.asarray(dft_tables()),
        )
    ]
    plane_pair = jax.ShapeDtypeStruct((2, W, W), F32)
    any_spec = pl.BlockSpec(memory_space=pltpu.HBM)
    smem_spec = pl.BlockSpec(memory_space=pltpu.SMEM)
    vmem_spec = pl.BlockSpec(memory_space=pltpu.VMEM)
    dma = pltpu.SemaphoreType.DMA
    scratch = [
        pltpu.VMEM((4, 4 * H, W), F32),
        pltpu.VMEM((4, 4 * H, W), F32),
        pltpu.VMEM((2, W, W), F32),
        pltpu.VMEM((slots, W, W), F32),
        pltpu.VMEM((HIST, 2, W, W), F32),
        pltpu.VMEM((HIST, 2, W, W), F32),
        pltpu.VMEM((2, W, W), F32),
        pltpu.VMEM((2, W, W), F32),
        pltpu.VMEM((4, 2 * W, 2 * W), BF16),
        pltpu.VMEM((GROUP, 2, W, W), F32),
        pltpu.VMEM((2 * W, GROUP * W), BF16),
        pltpu.VMEM((2 * W, GROUP * W), BF16),
        pltpu.VMEM((GROUP * W, 2 * W), BF16),
        pltpu.VMEM((GROUP * W, 2 * W), BF16),
        pltpu.VMEM((GROUP, 2, 3 * W, W), F32),
        pltpu.VMEM((2 * W, W), F32),
        pltpu.VMEM((2, 2, H, W), F32),
        pltpu.VMEM((2, 2, H, W), F32),
        pltpu.VMEM((4, H, W), F32),
        pltpu.VMEM((4, H, W), F32),
        pltpu.VMEM((4, 2, H, W), F32),
        pltpu.VMEM((4, H, W), F32),
        pltpu.VMEM((W, W), F32),
        pltpu.VMEM((W, W), F32),
        pltpu.VMEM((n_col - 1, part, W), F32),
        pltpu.VMEM((8 + part, W), F32),
        pltpu.VMEM((n_row - 1, 8 + part, W), F32),
        pltpu.VMEM((8 + 2 * part, W), F32),
        pltpu.VMEM((n_col - 1, 8 + 2 * part, W), F32),
        dma((7,)),
        dma((4,)),
        dma((4,)),
        dma((2,)),
        dma((2,)),
        dma((4,)),
        dma((4,)),
    ]
    og, direction, pg, nd = pl.pallas_call(
        functools.partial(kernel, n_row, n_col, slots),
        name="ptycho",
        out_shape=(plane_pair, plane_pair, jax.ShapeDtypeStruct((2 * W, W), F32), plane_pair),
        in_specs=[any_spec, any_spec, any_spec, smem_spec, smem_spec, any_spec, any_spec, any_spec, any_spec],
        out_specs=(vmem_spec,) * 4,
        scratch_shapes=scratch,
        compiler_params=pltpu.CompilerParams(
            collective_id=0, has_side_effects=True, vmem_limit_bytes=40 * 2**20
        ),
    )(
        object_tiles,
        probe,
        amplitudes,
        offsets,
        counts,
        past_steps,
        past_diffs,
        last_gradient,
        tables,
    )
    return pl.pallas_call(
        store,
        name="store",
        out_shape=(plane_pair,) * 4,
        in_specs=[vmem_spec] * 4,
        out_specs=(any_spec,) * 4,
        scratch_shapes=[dma((4,))],
        compiler_params=pltpu.CompilerParams(vmem_limit_bytes=2**20),
    )(og, direction, pg.reshape(2, W, W), nd)


def solution(mesh):
    return jax.shard_map(
        functools.partial(body, mesh.shape["row"], mesh.shape["col"]),
        mesh=mesh,
        in_specs=(
            P(None, "row", "col"),
            P(),
            P(("row", "col"), None, None),
            P(("row", "col"), None),
            P("row", "col"),
            P(None, None, "row", "col"),
            P(None, None, "row", "col"),
            P(None, "row", "col"),
        ),
        out_specs=(P(None, "row", "col"), P(None, "row", "col"), P(), P(None, "row", "col")),
        check_vma=False,
    )
```

```python
import functools
import math

import jax
import jax.numpy as jnp
import numpy as np
from jax import lax
from jax.experimental import pallas as pl
from jax.experimental.pallas import tpu as pltpu
from jax.sharding import PartitionSpec as P

MESH = pl.DeviceIdType.MESH
F32 = jnp.float32
BF16 = jnp.bfloat16
W = 128
H = W // 2
SOFTEN = 0.25
GROUP = 16
HIST = 4

NORTH, SOUTH, WEST, EAST = (-1, 0), (1, 0), (0, -1), (0, 1)
NW, NE, SW, SE = (-1, -1), (-1, 1), (1, -1), (1, 1)
AROUND = (NORTH, SOUTH, WEST, EAST, NW, NE, SW, SE)
SIDES = AROUND[:4]
CORNERS = AROUND[4:]

PAIRS_SY = [(i, j) for i in range(HIST) for j in range(i, HIST)]
PAIRS_YY = [(i, j) for i in range(HIST) for j in range(i, HIST)]
ROW_SY = {pair: n for n, pair in enumerate(PAIRS_SY)}
ROW_YY = {pair: len(PAIRS_SY) + n for n, pair in enumerate(PAIRS_YY)}
ROW_COUNT = len(PAIRS_SY) + len(PAIRS_YY)
ROW_SG = ROW_COUNT + 1
ROW_YG = ROW_SG + HIST
N_DOTS = ROW_YG + HIST


def dft_tables():
    index = np.arange(W)
    angle = (index[:, None] * index[None, :] % W) * (2.0 * math.pi / W)
    cosine = np.cos(angle) / math.sqrt(W)
    sine = np.sin(angle) / math.sqrt(W)
    return np.stack([cosine, sine]).astype(np.float32)


def split(x):
    high = x.astype(BF16)
    return high, (x - high.astype(F32)).astype(BF16)


def mm(a, b):
    return jnp.dot(a, b, preferred_element_type=F32)


def kernel(
    n_row,
    n_col,
    slots,
    obj,
    probe,
    amp,
    off_hbm,
    cnt,
    steps,
    diffs,
    last,
    tabs,
    og_ref,
    dir_ref,
    pg_ref,
    nd_ref,
    pad,
    grad,
    pr_v,
    amp_v,
    s_v,
    y_v,
    last_v,
    trig,
    tab,
    patches,
    xh,
    xl,
    ah,
    al,
    zed,
    pacc,
    side_out,
    side_in,
    corner_out,
    corner_in,
    gside_in,
    gcorner_in,
    dots,
    half_in,
    rs_in,
    grams,
    mix,
    row_in,
    mix2,
    col_in,
    off,
    loc_sem,
    halo_send,
    halo_recv,
    ghalo_send,
    ghalo_recv,
    sum_send,
    sum_recv,
):
    a = lax.axis_index("row")
    b = lax.axis_index("col")

    def at(step):
        return (lax.rem(a + step[0] % n_row, n_row), lax.rem(b + step[1] % n_col, n_col))

    def send(src, dst, send_sem, recv_sem, device):
        pltpu.make_async_remote_copy(
            src_ref=src,
            dst_ref=dst,
            send_sem=send_sem,
            recv_sem=recv_sem,
            device_id=device,
            device_id_type=MESH,
        ).start()

    def zero_at(index, edge):
        return jnp.where(index == edge, F32(0.0), F32(1.0))

    keep = {NORTH: zero_at(a, 0), SOUTH: zero_at(a, n_row - 1), WEST: zero_at(b, 0), EAST: zero_at(b, n_col - 1)}
    for dr, dc in CORNERS:
        keep[dr, dc] = keep[dr, 0] * keep[0, dc]

    core = lax.rem(a, 2)
    mate = (a + 1 - 2 * core, b)
    obj_copy = pltpu.make_async_copy(obj, pad.at[0:2, H : H + W], loc_sem.at[0])
    obj_copy.start()
    partners = [(dr % n_row, dc % n_col) for dr, dc in AROUND]
    others = [(d, 0) for d in range(1, n_row)] + [(0, d) for d in range(1, n_col)]
    partners += [step for step in others if step not in partners]
    barrier = pltpu.get_barrier_semaphore()
    for step in partners:
        pl.semaphore_signal(barrier, inc=1, device_id=at(step), device_id_type=MESH)
    local = []
    for n, (src, dst) in enumerate(
        ((steps, s_v), (diffs, y_v), (tabs, trig), (probe, pr_v), (amp, amp_v), (last, last_v), (off_hbm, off))
    ):
        copy = pltpu.make_async_copy(src, dst, loc_sem.at[n + 1])
        copy.start()
        local.append(copy)

    def drain(ref, sem):
        pltpu.make_async_copy(ref, ref, sem).wait()

    lane = lax.broadcasted_iota(jnp.int32, (H, W), 1)
    low = lane < H

    def turn(x):
        return pltpu.roll(x, H, 1)

    def pack(first, second):
        return jnp.where(low, first, second)

    obj_copy.wait()
    top = [pad[p, H : 2 * H] for p in range(2)]
    bottom = [pad[p, 2 * H : 3 * H] for p in range(2)]
    for p in range(2):
        side_out[0, p] = pack(top[p], turn(bottom[p]))
        side_out[1, p] = pack(turn(top[p]), bottom[p])
    for n, (dr, dc) in enumerate(CORNERS):
        rows = top if dr < 0 else bottom
        if dc < 0:
            corner_out[n] = pack(rows[0], turn(rows[1]))
        else:
            corner_out[n] = pack(turn(rows[0]), rows[1])

    pl.semaphore_wait(barrier, len(partners))

    for n, step in enumerate(CORNERS):
        send(corner_out.at[n], corner_in.at[n], halo_send.at[1], halo_recv.at[1], at(step))
    for n, step in enumerate((WEST, EAST)):
        send(side_out.at[n], side_in.at[n], halo_send.at[0], halo_recv.at[0], at(step))
    first_rows, last_rows = pad.at[0:2, 0:H], pad.at[0:2, 3 * H : 4 * H]
    send(pad.at[0:2, H : 2 * H], last_rows, halo_send.at[2], halo_recv.at[2], at(NORTH))
    send(pad.at[0:2, 2 * H : 3 * H], first_rows, halo_send.at[3], halo_recv.at[3], at(SOUTH))

    for copy in local[:2]:
        copy.wait()
    dots[...] = jnp.zeros_like(dots)
    flat = 2 * W

    def gram(n, sums):
        plane = n // (W // 8)
        rows = pl.ds(pl.multiple_of(lax.rem(n, W // 8) * 8, 8), 8)
        s = [s_v[i, plane, rows] for i in range(HIST)]
        y = [y_v[i, plane, rows] for i in range(HIST)]
        products = [s[i] * y[j] for i, j in PAIRS_SY] + [y[i] * y[j] for i, j in PAIRS_YY]
        return tuple(total + one for total, one in zip(sums, products))

    sums = lax.fori_loop(0, flat // 8, gram, (jnp.zeros((8, W), F32),) * ROW_COUNT, unroll=2)
    for n in range(ROW_COUNT):
        dots[n : n + 1] = jnp.sum(sums[n], 0, keepdims=True)
    local[6].wait()
    live_count = cnt[0, 0]
    lane_row = lax.broadcasted_iota(jnp.int32, (1, W), 1)
    dots[ROW_COUNT : ROW_COUNT + 1] = jnp.where(lane_row == 0, live_count, 0).astype(F32)
    grams[...] = lax.dot_general(
        jnp.ones((8, W), F32),
        dots[...],
        (((1,), (1,)), ((), ())),
        precision=lax.Precision.HIGHEST,
        preferred_element_type=F32,
    )

    local[2].wait()
    parts = [split(trig[n]) for n in range(2)]
    for n in range(2):
        cosine, sine = parts[0][n], parts[1][n]
        for base, above, below in ((0, sine, -sine), (2, -sine, sine)):
            tab[base + n, 0:W, 0:W] = cosine
            tab[base + n, W:, W:] = cosine
            tab[base + n, 0:W, W:] = above
            tab[base + n, W:, 0:W] = below

    grad[...] = jnp.zeros_like(grad)
    pacc[...] = jnp.zeros_like(pacc)
    zed[...] = jnp.zeros_like(zed)

    for copy in local[3:5]:
        copy.wait()
    for sems in (halo_send, halo_recv):
        for n, ref in enumerate((side_in, corner_in, last_rows, first_rows)):
            drain(ref, sems.at[n])

    for p in range(2):
        pad[p, 0:H] = pad[p, 0:H] * keep[NORTH]
        pad[p, 3 * H : 4 * H] = pad[p, 3 * H : 4 * H] * keep[SOUTH]
        east = side_in[0, p] * keep[EAST]
        west = side_in[1, p] * keep[WEST]
        pad[2 + p, H : 2 * H] = pack(east, turn(west))
        pad[2 + p, 2 * H : 3 * H] = pack(turn(east), west)
    for rows, side in ((slice(0, H), -1), (slice(3 * H, 4 * H), 1)):
        from_east = corner_in[CORNERS.index((-side, -1))] * keep[side, 1]
        from_west = corner_in[CORNERS.index((-side, 1))] * keep[side, -1]
        pad[2, rows] = pack(from_east, turn(from_west))
        pad[3, rows] = pack(turn(from_east), from_west)

    lanes = lax.broadcasted_iota(jnp.int32, (W, W), 1)
    lanes_h = lax.broadcasted_iota(jnp.int32, (H, W), 1)

    def own(q, iota):
        return (iota >= jnp.maximum(q, 0)) & (iota < jnp.minimum(q + W, W))

    def group(g, carry):
        first = g * GROUP
        offs = []
        for j in range(GROUP):
            k = first + j
            r, c = off[0, k], off[1, k]
            offs.append((r, c))
            inside = own(c - H, lanes)
            part = []
            for p in range(2):
                here = pad[p, pl.ds(r, W)]
                beside = pad[2 + p, pl.ds(r, W)]
                part.append(pltpu.roll(jnp.where(inside, here, beside), lax.rem(W + H - c, W), 1))
                patches[j, p] = part[p]
            pr, pi = pr_v[0], pr_v[1]
            cols = slice(j * W, (j + 1) * W)
            xh[0:W, cols], xl[0:W, cols] = split(pr * part[0] - pi * part[1])
            xh[W : 2 * W, cols], xl[W : 2 * W, cols] = split(pr * part[1] + pi * part[0])

        def left(high, low_part, emit):
            for h in range(GROUP // 2):
                cols = slice(h * 2 * W, (h + 1) * 2 * W)
                out = mm(high, xh[:, cols]) + mm(low_part, xh[:, cols]) + mm(high, xl[:, cols])
                for i in range(2):
                    emit(2 * h + i, out[0:W, i * W : (i + 1) * W], out[W:, i * W : (i + 1) * W])

        def right(high, low_part, emit):
            for h in range(GROUP // 2):
                rows = slice(h * 2 * W, (h + 1) * 2 * W)
                out = mm(ah[rows], high) + mm(ah[rows], low_part) + mm(al[rows], high)
                for i in range(2):
                    emit(2 * h + i, out[i * W : (i + 1) * W, 0:W], out[i * W : (i + 1) * W, W:])

        def to_rows(j, real, imag):
            rows = slice(j * W, (j + 1) * W)
            ah[rows, 0:W], al[rows, 0:W] = split(real)
            ah[rows, W:], al[rows, W:] = split(imag)

        def to_cols(j, real, imag):
            cols = slice(j * W, (j + 1) * W)
            xh[0:W, cols], xl[0:W, cols] = split(real)
            xh[W:, cols], xl[W:, cols] = split(imag)

        def weigh(j, real, imag):
            inverse = lax.rsqrt(real * real + imag * imag + SOFTEN)
            live = jnp.where(first + j < live_count, F32(2.0), F32(0.0))
            factor = live * (1.0 - amp_v[first + j] * inverse)
            to_rows(j, factor * real, factor * imag)

        def finish(j, real, imag):
            r, c = offs[j]
            pr, pi = pr_v[0], pr_v[1]
            shift = lax.rem(c + H, W)
            zed[j, 0, W : 2 * W] = pltpu.roll(pr * real + pi * imag, shift, 1)
            zed[j, 1, W : 2 * W] = pltpu.roll(pr * imag - pi * real, shift, 1)
            o_re, o_im = patches[j, 0], patches[j, 1]
            pacc[0:W] += o_re * real + o_im * imag
            pacc[W:] += o_re * imag - o_im * real

        left(tab[0], tab[1], to_rows)
        right(tab[2], tab[3], weigh)
        right(tab[0], tab[1], to_cols)
        left(tab[2], tab[3], finish)

        inside = [own(c - H, lanes_h) for _, c in offs]
        for ch in range(4):
            rows = slice(ch * H, (ch + 1) * H)
            for p in range(2):
                here, beside = grad[p, rows], grad[2 + p, rows]
                for j in range(GROUP):
                    moved = zed[j, p, pl.ds(W - offs[j][0] + ch * H, H)]
                    here += jnp.where(inside[j], moved, 0.0)
                    beside += jnp.where(inside[j], 0.0, moved)
                grad[p, rows], grad[2 + p, rows] = here, beside
        return carry

    lax.fori_loop(0, slots // GROUP, group, 0)

    other_plane = pl.ds(pl.multiple_of((1 - core) * W, W), W)
    send(pacc.at[other_plane], half_in, sum_send.at[0], sum_recv.at[0], mate)

    for p in range(2):
        upper, lower = grad[2 + p, H : 2 * H], grad[2 + p, 2 * H : 3 * H]
        side_out[0, p] = pack(turn(upper), lower)
        side_out[1, p] = pack(upper, turn(lower))
    for n, (dr, dc) in enumerate(CORNERS):
        rows = slice(0, H) if dr < 0 else slice(3 * H, 4 * H)
        first, second = grad[2, rows], grad[3, rows]
        corner_out[n] = pack(turn(first), second) if dc < 0 else pack(first, turn(second))
    for n, step in enumerate(CORNERS):
        send(corner_out.at[n], gcorner_in.at[n], ghalo_send.at[1], ghalo_recv.at[1], at(step))
    for n, (src, step) in enumerate(
        (
            (side_out.at[0], WEST),
            (side_out.at[1], EAST),
            (grad.at[0:2, 0:H], NORTH),
            (grad.at[0:2, 3 * H : 4 * H], SOUTH),
        )
    ):
        send(src, gside_in.at[n], ghalo_send.at[0], ghalo_recv.at[0], at(step))

    part = W // n_col

    def plane_rows(plane, start, size):
        return pl.ds(pl.multiple_of(plane * W + start, 8), size)

    drain(half_in, sum_recv.at[0])
    pacc[plane_rows(core, 0, W)] += half_in[...]
    for d in range(1, n_col):
        rows = plane_rows(core, lax.rem(b + d, n_col) * part, part)
        send(pacc.at[rows], rs_in.at[d - 1], sum_send.at[1], sum_recv.at[1], at((0, d)))

    drain(gside_in, ghalo_recv.at[0])
    drain(gcorner_in, ghalo_recv.at[1])
    for p in range(2):
        east, west = gside_in[0, p] * keep[EAST], gside_in[1, p] * keep[WEST]
        for side, mid in ((-1, pack(west, turn(east))), (1, pack(turn(west), east))):
            from_east = gcorner_in[CORNERS.index((-side, -1))] * keep[side, 1]
            from_west = gcorner_in[CORNERS.index((-side, 1))] * keep[side, -1]
            if p == 0:
                corner = pack(from_west, turn(from_east))
            else:
                corner = pack(turn(from_west), from_east)
            vertical = gside_in[3 if side < 0 else 2, p] * keep[side, 0]
            mine = grad[p, H : 2 * H] if side < 0 else grad[p, 2 * H : 3 * H]
            if side < 0:
                og_ref[p, 0:H] = mine + vertical + mid + corner
            else:
                og_ref[p, H:] = mine + vertical + mid + corner

    def with_gradient(n, sums):
        plane = n // (W // 8)
        rows = pl.ds(pl.multiple_of(lax.rem(n, W // 8) * 8, 8), 8)
        g = og_ref[plane, rows]
        products = [s_v[i, plane, rows] * g for i in range(HIST)] + [y_v[i, plane, rows] * g for i in range(HIST)]
        return tuple(total + one for total, one in zip(sums, products))

    sums = lax.fori_loop(
        0, flat // 8, with_gradient, (jnp.zeros((8, W), F32),) * (2 * HIST), unroll=8
    )
    row8 = lax.broadcasted_iota(jnp.int32, (8, W), 0)
    lane8 = lax.broadcasted_iota(jnp.int32, (8, W), 1)
    inner = jnp.zeros((8, W), F32)
    for n in range(2 * HIST):
        inner = jnp.where(row8 == n, jnp.sum(sums[n], 0, keepdims=True), inner)
    inner = jnp.sum(inner, 1, keepdims=True)
    inner = jnp.where(lane8 == ROW_SG + row8, inner, jnp.where(row8 == 0, grams[...], 0.0))
    mix[0] = jnp.sum(inner, 0, keepdims=True)

    drain(rs_in, sum_recv.at[1])
    total = pacc[plane_rows(core, b * part, part)]
    for d in range(n_col - 1):
        total += rs_in[d]
    for n in range(part):
        mix[1 + n] = total[n : n + 1]

    for d in range(1, n_row):
        send(mix, row_in.at[d - 1], sum_send.at[2], sum_recv.at[2], at((d, 0)))
    drain(half_in, sum_send.at[0])
    drain(rs_in, sum_send.at[1])
    drain(gside_in, ghalo_send.at[0])
    drain(gcorner_in, ghalo_send.at[1])
    drain(row_in, sum_recv.at[2])
    own, odd = mix[...], row_in[0]
    for d in range(2, n_row):
        if d % 2 == 0:
            own += row_in[d - 1]
        else:
            odd += row_in[d - 1]
    mix2[0] = own[0] + odd[0]
    mix2[1 : 1 + part] = own[1:]
    mix2[1 + part :] = odd[1:]

    for d in range(1, n_col):
        send(mix2, col_in.at[d - 1], sum_send.at[3], sum_recv.at[3], at((0, d)))
    drain(row_in, sum_send.at[2])
    local[5].wait()
    drain(col_in, sum_recv.at[3])
    total = mix2[0]
    for d in range(n_col - 1):
        total += col_in[d, 0]
    total = jnp.broadcast_to(total, (8, W))

    value = [jnp.broadcast_to(total[:, n : n + 1], (8, W)) for n in range(N_DOTS)]
    live_total = value[ROW_COUNT]
    per_live = 1.0 / live_total
    scale = (n_row * n_col) * per_live
    sg = [value[ROW_SG + i] * scale for i in range(HIST)]
    yg = [value[ROW_YG + i] * scale for i in range(HIST)]
    rho = [1.0 / value[ROW_SY[i, i]] for i in range(HIST)]
    alpha = [None] * HIST
    for i in reversed(range(HIST)):
        inner = sg[i]
        for j in range(i + 1, HIST):
            inner = inner - alpha[j] * value[ROW_SY[i, j]]
        alpha[i] = rho[i] * inner
    gamma = value[ROW_SY[HIST - 1, HIST - 1]] / value[ROW_YY[HIST - 1, HIST - 1]]
    weight = [None] * HIST
    for i in range(HIST):
        inner = yg[i]
        for j in range(HIST):
            inner = inner - alpha[j] * value[ROW_YY[min(i, j), max(i, j)]]
        inner = gamma * inner
        for j in range(i):
            inner = inner + weight[j] * value[ROW_SY[j, i]]
        weight[i] = alpha[i] - rho[i] * inner

    def finish_rows(n, carry):
        plane = n // (W // 8)
        rows = pl.ds(pl.multiple_of(lax.rem(n, W // 8) * 8, 8), 8)
        g = og_ref[plane, rows] * scale
        og_ref[plane, rows] = g
        nd_ref[plane, rows] = g - last_v[plane, rows]
        q = g
        for i in range(HIST):
            q = q - alpha[i] * y_v[i, plane, rows]
        q = gamma * q
        for i in range(HIST):
            q = q + weight[i] * s_v[i, plane, rows]
        dir_ref[plane, rows] = -q
        return carry

    lax.fori_loop(0, flat // 8, finish_rows, 0, unroll=8)

    weight_live = per_live[0:1]
    for d in range(n_col):
        col = lax.rem(b + n_col - d, n_col) * part
        found = mix2 if d == 0 else col_in.at[d - 1]
        for half in range(2):
            parts = [found[1 + half * part + n] * weight_live for n in range(part)]
            pg_ref[plane_rows(core if half == 0 else 1 - core, col, part)] = jnp.concatenate(parts, 0)
    drain(col_in, sum_send.at[3])


def store(a, b, c, d, a_out, b_out, c_out, d_out, sem):
    copies = [
        pltpu.make_async_copy(src, dst, sem.at[n])
        for n, (src, dst) in enumerate(((a, a_out), (b, b_out), (c, c_out), (d, d_out)))
    ]
    for copy in copies:
        copy.start()
    for copy in copies:
        copy.wait()


def body(n_row, n_col, object_tiles, probe, amplitudes, offsets, counts, past_steps, past_diffs, last_gradient):
    slots = amplitudes.shape[0]
    part = W // n_col
    object_tiles, probe, amplitudes, offsets, past_steps, past_diffs, last_gradient, tables = [
        pltpu.with_memory_space_constraint(x, pltpu.HBM)
        for x in (
            object_tiles,
            probe,
            amplitudes,
            offsets.T,
            past_steps,
            past_diffs,
            last_gradient,
            jnp.asarray(dft_tables()),
        )
    ]
    plane_pair = jax.ShapeDtypeStruct((2, W, W), F32)
    any_spec = pl.BlockSpec(memory_space=pltpu.HBM)
    vmem_spec = pl.BlockSpec(memory_space=pltpu.VMEM)
    dma = pltpu.SemaphoreType.DMA
    scratch = [
        pltpu.VMEM((4, 4 * H, W), F32),
        pltpu.VMEM((4, 4 * H, W), F32),
        pltpu.VMEM((2, W, W), F32),
        pltpu.VMEM((slots, W, W), F32),
        pltpu.VMEM((HIST, 2, W, W), F32),
        pltpu.VMEM((HIST, 2, W, W), F32),
        pltpu.VMEM((2, W, W), F32),
        pltpu.VMEM((2, W, W), F32),
        pltpu.VMEM((4, 2 * W, 2 * W), BF16),
        pltpu.VMEM((GROUP, 2, W, W), F32),
        pltpu.VMEM((2 * W, GROUP * W), BF16),
        pltpu.VMEM((2 * W, GROUP * W), BF16),
        pltpu.VMEM((GROUP * W, 2 * W), BF16),
        pltpu.VMEM((GROUP * W, 2 * W), BF16),
        pltpu.VMEM((GROUP, 2, 3 * W, W), F32),
        pltpu.VMEM((2 * W, W), F32),
        pltpu.VMEM((2, 2, H, W), F32),
        pltpu.VMEM((2, 2, H, W), F32),
        pltpu.VMEM((4, H, W), F32),
        pltpu.VMEM((4, H, W), F32),
        pltpu.VMEM((4, 2, H, W), F32),
        pltpu.VMEM((4, H, W), F32),
        pltpu.VMEM((W, W), F32),
        pltpu.VMEM((W, W), F32),
        pltpu.VMEM((n_col - 1, part, W), F32),
        pltpu.VMEM((8, W), F32),
        pltpu.VMEM((1 + part, 1, W), F32),
        pltpu.VMEM((n_row - 1, 1 + part, 1, W), F32),
        pltpu.VMEM((1 + 2 * part, 1, W), F32),
        pltpu.VMEM((n_col - 1, 1 + 2 * part, 1, W), F32),
        pltpu.SMEM((2, slots), jnp.int32),
        dma((8,)),
        dma((4,)),
        dma((4,)),
        dma((2,)),
        dma((2,)),
        dma((4,)),
        dma((4,)),
    ]
    og, direction, pg, nd = pl.pallas_call(
        functools.partial(kernel, n_row, n_col, slots),
        name="ptycho",
        out_shape=(plane_pair, plane_pair, jax.ShapeDtypeStruct((2 * W, W), F32), plane_pair),
        in_specs=[any_spec] * 4 + [pl.BlockSpec(memory_space=pltpu.SMEM)] + [any_spec] * 4,
        out_specs=(vmem_spec,) * 4,
        scratch_shapes=scratch,
        compiler_params=pltpu.CompilerParams(
            collective_id=0, has_side_effects=True, vmem_limit_bytes=40 * 2**20
        ),
    )(
        object_tiles,
        probe,
        amplitudes,
        offsets,
        counts,
        past_steps,
        past_diffs,
        last_gradient,
        tables,
    )
    return pl.pallas_call(
        store,
        name="store",
        out_shape=(plane_pair,) * 4,
        in_specs=[vmem_spec] * 4,
        out_specs=(any_spec,) * 4,
        scratch_shapes=[dma((4,))],
        compiler_params=pltpu.CompilerParams(vmem_limit_bytes=2**20),
    )(og, direction, pg.reshape(2, W, W), nd)


def solution(mesh):
    return jax.shard_map(
        functools.partial(body, mesh.shape["row"], mesh.shape["col"]),
        mesh=mesh,
        in_specs=(
            P(None, "row", "col"),
            P(),
            P(("row", "col"), None, None),
            P(("row", "col"), None),
            P("row", "col"),
            P(None, None, "row", "col"),
            P(None, None, "row", "col"),
            P(None, "row", "col"),
        ),
        out_specs=(P(None, "row", "col"), P(None, "row", "col"), P(), P(None, "row", "col")),
        check_vma=False,
    )
```

```python
import functools
import math

import jax
import jax.numpy as jnp
import numpy as np
from jax import lax
from jax.experimental import pallas as pl
from jax.experimental.pallas import tpu as pltpu
from jax.sharding import PartitionSpec as P

MESH = pl.DeviceIdType.MESH
F32 = jnp.float32
BF16 = jnp.bfloat16
W = 128
H = W // 2
SOFTEN = 0.25
GROUP = 16
HIST = 4

NORTH, SOUTH, WEST, EAST = (-1, 0), (1, 0), (0, -1), (0, 1)
NW, NE, SW, SE = (-1, -1), (-1, 1), (1, -1), (1, 1)
AROUND = (NORTH, SOUTH, WEST, EAST, NW, NE, SW, SE)
SIDES = AROUND[:4]
CORNERS = AROUND[4:]

PAIRS_SY = [(i, j) for i in range(HIST) for j in range(i, HIST)]
PAIRS_YY = [(i, j) for i in range(HIST) for j in range(i, HIST)]
ROW_SY = {pair: n for n, pair in enumerate(PAIRS_SY)}
ROW_YY = {pair: len(PAIRS_SY) + n for n, pair in enumerate(PAIRS_YY)}
ROW_COUNT = len(PAIRS_SY) + len(PAIRS_YY)
ROW_SG = ROW_COUNT + 1
ROW_YG = ROW_SG + HIST
N_DOTS = ROW_YG + HIST


def dft_tables():
    index = np.arange(W)
    angle = (index[:, None] * index[None, :] % W) * (2.0 * math.pi / W)
    cosine = np.cos(angle) / math.sqrt(W)
    sine = np.sin(angle) / math.sqrt(W)
    return np.stack([cosine, sine]).astype(np.float32)


def farthest_first(count):
    return sorted(range(1, count), key=lambda d: -min(d, count - d))


def split(x):
    high = x.astype(BF16)
    return high, (x - high.astype(F32)).astype(BF16)


def mm(a, b):
    return jnp.dot(a, b, preferred_element_type=F32)


def kernel(
    n_row,
    n_col,
    slots,
    obj,
    probe,
    amp,
    off_hbm,
    cnt,
    steps,
    diffs,
    last,
    tabs,
    og_ref,
    dir_ref,
    pg_ref,
    nd_ref,
    pad,
    grad,
    pr_v,
    amp_v,
    s_v,
    y_v,
    last_v,
    trig,
    tab,
    patches,
    xh,
    xl,
    ah,
    al,
    zed,
    pacc,
    side_out,
    side_in,
    corner_out,
    corner_in,
    gside_in,
    gcorner_in,
    dots,
    half_in,
    rs_in,
    grams,
    mix,
    row_in,
    mix2,
    col_in,
    off,
    loc_sem,
    halo_send,
    halo_recv,
    ghalo_send,
    ghalo_recv,
    sum_send,
    sum_recv,
    reach,
):
    a = lax.axis_index("row")
    b = lax.axis_index("col")

    def at(step):
        return (lax.rem(a + step[0] % n_row, n_row), lax.rem(b + step[1] % n_col, n_col))

    def send(src, dst, send_sem, recv_sem, device):
        pltpu.make_async_remote_copy(
            src_ref=src,
            dst_ref=dst,
            send_sem=send_sem,
            recv_sem=recv_sem,
            device_id=device,
            device_id_type=MESH,
        ).start()

    def zero_at(index, edge):
        return jnp.where(index == edge, F32(0.0), F32(1.0))

    keep = {NORTH: zero_at(a, 0), SOUTH: zero_at(a, n_row - 1), WEST: zero_at(b, 0), EAST: zero_at(b, n_col - 1)}
    for dr, dc in CORNERS:
        keep[dr, dc] = keep[dr, 0] * keep[0, dc]

    core = lax.rem(a, 2)
    mate = (a + 1 - 2 * core, b)
    obj_copy = pltpu.make_async_copy(obj, pad.at[0:2, H : H + W], loc_sem.at[0])
    obj_copy.start()
    barrier = pltpu.get_barrier_semaphore()
    for step in CORNERS + SIDES:
        pl.semaphore_signal(barrier, inc=1, device_id=at(step), device_id_type=MESH)
    local = []
    for n, (src, dst) in enumerate(
        ((steps, s_v), (diffs, y_v), (tabs, trig), (probe, pr_v), (amp, amp_v), (last, last_v), (off_hbm, off))
    ):
        copy = pltpu.make_async_copy(src, dst, loc_sem.at[n + 1])
        copy.start()
        local.append(copy)

    def drain(ref, sem):
        pltpu.make_async_copy(ref, ref, sem).wait()

    lane = lax.broadcasted_iota(jnp.int32, (H, W), 1)
    low = lane < H

    def turn(x):
        return pltpu.roll(x, H, 1)

    def pack(first, second):
        return jnp.where(low, first, second)

    obj_copy.wait()
    top = [pad[p, H : 2 * H] for p in range(2)]
    bottom = [pad[p, 2 * H : 3 * H] for p in range(2)]
    for p in range(2):
        side_out[0, p] = pack(top[p], turn(bottom[p]))
        side_out[1, p] = pack(turn(top[p]), bottom[p])
    for n, (dr, dc) in enumerate(CORNERS):
        rows = top if dr < 0 else bottom
        if dc < 0:
            corner_out[n] = pack(rows[0], turn(rows[1]))
        else:
            corner_out[n] = pack(turn(rows[0]), rows[1])

    pl.semaphore_wait(barrier, len(AROUND))

    def tell(n):
        for step in SIDES:
            device = at((step[0] * 2**n, step[1] * 2**n))
            pl.semaphore_signal(reach.at[n], inc=1, device_id=device, device_id_type=MESH)

    def hear(n):
        pl.semaphore_wait(reach.at[n], len(SIDES))


    for n, step in enumerate(CORNERS):
        send(corner_out.at[n], corner_in.at[n], halo_send.at[1], halo_recv.at[1], at(step))
    for n, step in enumerate((WEST, EAST)):
        send(side_out.at[n], side_in.at[n], halo_send.at[0], halo_recv.at[0], at(step))
    first_rows, last_rows = pad.at[0:2, 0:H], pad.at[0:2, 3 * H : 4 * H]
    send(pad.at[0:2, H : 2 * H], last_rows, halo_send.at[2], halo_recv.at[2], at(NORTH))
    send(pad.at[0:2, 2 * H : 3 * H], first_rows, halo_send.at[3], halo_recv.at[3], at(SOUTH))

    tell(0)

    for copy in local[:2]:
        copy.wait()
    dots[...] = jnp.zeros_like(dots)
    flat = 2 * W

    def gram(n, sums):
        plane = n // (W // 8)
        rows = pl.ds(pl.multiple_of(lax.rem(n, W // 8) * 8, 8), 8)
        s = [s_v[i, plane, rows] for i in range(HIST)]
        y = [y_v[i, plane, rows] for i in range(HIST)]
        products = [s[i] * y[j] for i, j in PAIRS_SY] + [y[i] * y[j] for i, j in PAIRS_YY]
        return tuple(total + one for total, one in zip(sums, products))

    sums = lax.fori_loop(0, flat // 8, gram, (jnp.zeros((8, W), F32),) * ROW_COUNT, unroll=2)
    for n in range(ROW_COUNT):
        dots[n : n + 1] = jnp.sum(sums[n], 0, keepdims=True)
    local[6].wait()
    live_count = cnt[0, 0]
    lane_row = lax.broadcasted_iota(jnp.int32, (1, W), 1)
    dots[ROW_COUNT : ROW_COUNT + 1] = jnp.where(lane_row == 0, live_count, 0).astype(F32)
    grams[...] = lax.dot_general(
        jnp.ones((8, W), F32),
        dots[...],
        (((1,), (1,)), ((), ())),
        precision=lax.Precision.HIGHEST,
        preferred_element_type=F32,
    )

    hear(0)
    tell(1)
    local[2].wait()
    parts = [split(trig[n]) for n in range(2)]
    for n in range(2):
        cosine, sine = parts[0][n], parts[1][n]
        for base, above, below in ((0, sine, -sine), (2, -sine, sine)):
            tab[base + n, 0:W, 0:W] = cosine
            tab[base + n, W:, W:] = cosine
            tab[base + n, 0:W, W:] = above
            tab[base + n, W:, 0:W] = below

    grad[...] = jnp.zeros_like(grad)
    pacc[...] = jnp.zeros_like(pacc)
    zed[...] = jnp.zeros_like(zed)

    hear(1)
    tell(2)
    for copy in local[3:5]:
        copy.wait()
    for sems in (halo_send, halo_recv):
        for n, ref in enumerate((side_in, corner_in, last_rows, first_rows)):
            drain(ref, sems.at[n])

    for p in range(2):
        pad[p, 0:H] = pad[p, 0:H] * keep[NORTH]
        pad[p, 3 * H : 4 * H] = pad[p, 3 * H : 4 * H] * keep[SOUTH]
        east = side_in[0, p] * keep[EAST]
        west = side_in[1, p] * keep[WEST]
        pad[2 + p, H : 2 * H] = pack(east, turn(west))
        pad[2 + p, 2 * H : 3 * H] = pack(turn(east), west)
    for rows, side in ((slice(0, H), -1), (slice(3 * H, 4 * H), 1)):
        from_east = corner_in[CORNERS.index((-side, -1))] * keep[side, 1]
        from_west = corner_in[CORNERS.index((-side, 1))] * keep[side, -1]
        pad[2, rows] = pack(from_east, turn(from_west))
        pad[3, rows] = pack(turn(from_east), from_west)

    lanes = lax.broadcasted_iota(jnp.int32, (W, W), 1)
    lanes_h = lax.broadcasted_iota(jnp.int32, (H, W), 1)

    def own(q, iota):
        return (iota >= jnp.maximum(q, 0)) & (iota < jnp.minimum(q + W, W))

    def group(g, carry):
        first = g * GROUP
        offs = []
        for j in range(GROUP):
            k = first + j
            r, c = off[0, k], off[1, k]
            offs.append((r, c))
            inside = own(c - H, lanes)
            part = []
            for p in range(2):
                here = pad[p, pl.ds(r, W)]
                beside = pad[2 + p, pl.ds(r, W)]
                part.append(pltpu.roll(jnp.where(inside, here, beside), lax.rem(W + H - c, W), 1))
                patches[j, p] = part[p]
            pr, pi = pr_v[0], pr_v[1]
            cols = slice(j * W, (j + 1) * W)
            xh[0:W, cols], xl[0:W, cols] = split(pr * part[0] - pi * part[1])
            xh[W : 2 * W, cols], xl[W : 2 * W, cols] = split(pr * part[1] + pi * part[0])

        def left(high, low_part, emit):
            for h in range(GROUP // 2):
                cols = slice(h * 2 * W, (h + 1) * 2 * W)
                out = mm(high, xh[:, cols]) + mm(low_part, xh[:, cols]) + mm(high, xl[:, cols])
                for i in range(2):
                    emit(2 * h + i, out[0:W, i * W : (i + 1) * W], out[W:, i * W : (i + 1) * W])

        def right(high, low_part, emit):
            for h in range(GROUP // 2):
                rows = slice(h * 2 * W, (h + 1) * 2 * W)
                out = mm(ah[rows], high) + mm(ah[rows], low_part) + mm(al[rows], high)
                for i in range(2):
                    emit(2 * h + i, out[i * W : (i + 1) * W, 0:W], out[i * W : (i + 1) * W, W:])

        def to_rows(j, real, imag):
            rows = slice(j * W, (j + 1) * W)
            ah[rows, 0:W], al[rows, 0:W] = split(real)
            ah[rows, W:], al[rows, W:] = split(imag)

        def to_cols(j, real, imag):
            cols = slice(j * W, (j + 1) * W)
            xh[0:W, cols], xl[0:W, cols] = split(real)
            xh[W:, cols], xl[W:, cols] = split(imag)

        def weigh(j, real, imag):
            inverse = lax.rsqrt(real * real + imag * imag + SOFTEN)
            live = jnp.where(first + j < live_count, F32(2.0), F32(0.0))
            factor = live * (1.0 - amp_v[first + j] * inverse)
            to_rows(j, factor * real, factor * imag)

        def finish(j, real, imag):
            r, c = offs[j]
            pr, pi = pr_v[0], pr_v[1]
            shift = lax.rem(c + H, W)
            zed[j, 0, W : 2 * W] = pltpu.roll(pr * real + pi * imag, shift, 1)
            zed[j, 1, W : 2 * W] = pltpu.roll(pr * imag - pi * real, shift, 1)
            o_re, o_im = patches[j, 0], patches[j, 1]
            pacc[0:W] += o_re * real + o_im * imag
            pacc[W:] += o_re * imag - o_im * real

        left(tab[0], tab[1], to_rows)
        right(tab[2], tab[3], weigh)
        right(tab[0], tab[1], to_cols)
        left(tab[2], tab[3], finish)

        inside = [own(c - H, lanes_h) for _, c in offs]
        for ch in range(4):
            rows = slice(ch * H, (ch + 1) * H)
            for p in range(2):
                here, beside = grad[p, rows], grad[2 + p, rows]
                for j in range(GROUP):
                    moved = zed[j, p, pl.ds(W - offs[j][0] + ch * H, H)]
                    here += jnp.where(inside[j], moved, 0.0)
                    beside += jnp.where(inside[j], 0.0, moved)
                grad[p, rows], grad[2 + p, rows] = here, beside
        return carry

    lax.fori_loop(0, slots // GROUP, group, 0)

    other_plane = pl.ds(pl.multiple_of((1 - core) * W, W), W)
    send(pacc.at[other_plane], half_in, sum_send.at[0], sum_recv.at[0], mate)

    for p in range(2):
        upper, lower = grad[2 + p, H : 2 * H], grad[2 + p, 2 * H : 3 * H]
        side_out[0, p] = pack(turn(upper), lower)
        side_out[1, p] = pack(upper, turn(lower))
    for n, (dr, dc) in enumerate(CORNERS):
        rows = slice(0, H) if dr < 0 else slice(3 * H, 4 * H)
        first, second = grad[2, rows], grad[3, rows]
        corner_out[n] = pack(turn(first), second) if dc < 0 else pack(first, turn(second))
    for n, step in enumerate(CORNERS):
        send(corner_out.at[n], gcorner_in.at[n], ghalo_send.at[1], ghalo_recv.at[1], at(step))
    for n, (src, step) in enumerate(
        (
            (side_out.at[0], WEST),
            (side_out.at[1], EAST),
            (grad.at[0:2, 0:H], NORTH),
            (grad.at[0:2, 3 * H : 4 * H], SOUTH),
        )
    ):
        send(src, gside_in.at[n], ghalo_send.at[0], ghalo_recv.at[0], at(step))

    part = W // n_col

    def plane_rows(plane, start, size):
        return pl.ds(pl.multiple_of(plane * W + start, 8), size)

    hear(2)
    drain(half_in, sum_recv.at[0])
    pacc[plane_rows(core, 0, W)] += half_in[...]
    for d in farthest_first(n_col):
        rows = plane_rows(core, lax.rem(b + d, n_col) * part, part)
        send(pacc.at[rows], rs_in.at[d - 1], sum_send.at[1], sum_recv.at[1], at((0, d)))

    drain(gside_in, ghalo_recv.at[0])
    drain(gcorner_in, ghalo_recv.at[1])
    for p in range(2):
        east, west = gside_in[0, p] * keep[EAST], gside_in[1, p] * keep[WEST]
        for side, mid in ((-1, pack(west, turn(east))), (1, pack(turn(west), east))):
            from_east = gcorner_in[CORNERS.index((-side, -1))] * keep[side, 1]
            from_west = gcorner_in[CORNERS.index((-side, 1))] * keep[side, -1]
            if p == 0:
                corner = pack(from_west, turn(from_east))
            else:
                corner = pack(turn(from_west), from_east)
            vertical = gside_in[3 if side < 0 else 2, p] * keep[side, 0]
            mine = grad[p, H : 2 * H] if side < 0 else grad[p, 2 * H : 3 * H]
            if side < 0:
                og_ref[p, 0:H] = mine + vertical + mid + corner
            else:
                og_ref[p, H:] = mine + vertical + mid + corner

    def with_gradient(n, sums):
        plane = n // (W // 8)
        rows = pl.ds(pl.multiple_of(lax.rem(n, W // 8) * 8, 8), 8)
        g = og_ref[plane, rows]
        products = [s_v[i, plane, rows] * g for i in range(HIST)] + [y_v[i, plane, rows] * g for i in range(HIST)]
        return tuple(total + one for total, one in zip(sums, products))

    sums = lax.fori_loop(
        0, flat // 8, with_gradient, (jnp.zeros((8, W), F32),) * (2 * HIST), unroll=8
    )
    row8 = lax.broadcasted_iota(jnp.int32, (8, W), 0)
    lane8 = lax.broadcasted_iota(jnp.int32, (8, W), 1)
    inner = jnp.zeros((8, W), F32)
    for n in range(2 * HIST):
        inner = jnp.where(row8 == n, jnp.sum(sums[n], 0, keepdims=True), inner)
    inner = jnp.sum(inner, 1, keepdims=True)
    inner = jnp.where(lane8 == ROW_SG + row8, inner, jnp.where(row8 == 0, grams[...], 0.0))
    mix[0] = jnp.sum(inner, 0, keepdims=True)

    drain(rs_in, sum_recv.at[1])
    total = pacc[plane_rows(core, b * part, part)]
    for d in range(n_col - 1):
        total += rs_in[d]
    for n in range(part):
        mix[1 + n] = total[n : n + 1]

    for d in farthest_first(n_row):
        send(mix, row_in.at[d - 1], sum_send.at[2], sum_recv.at[2], at((d, 0)))
    drain(half_in, sum_send.at[0])
    drain(rs_in, sum_send.at[1])
    drain(gside_in, ghalo_send.at[0])
    drain(gcorner_in, ghalo_send.at[1])
    drain(row_in, sum_recv.at[2])
    own, odd = mix[...], row_in[0]
    for d in range(2, n_row):
        if d % 2 == 0:
            own += row_in[d - 1]
        else:
            odd += row_in[d - 1]
    mix2[0] = own[0] + odd[0]
    mix2[1 : 1 + part] = own[1:]
    mix2[1 + part :] = odd[1:]

    for d in farthest_first(n_col):
        send(mix2, col_in.at[d - 1], sum_send.at[3], sum_recv.at[3], at((0, d)))
    drain(row_in, sum_send.at[2])
    local[5].wait()
    drain(col_in, sum_recv.at[3])
    total = mix2[0]
    for d in range(n_col - 1):
        total += col_in[d, 0]
    total = jnp.broadcast_to(total, (8, W))

    value = [jnp.broadcast_to(total[:, n : n + 1], (8, W)) for n in range(N_DOTS)]
    live_total = value[ROW_COUNT]
    per_live = 1.0 / live_total
    scale = (n_row * n_col) * per_live
    sg = [value[ROW_SG + i] * scale for i in range(HIST)]
    yg = [value[ROW_YG + i] * scale for i in range(HIST)]
    rho = [1.0 / value[ROW_SY[i, i]] for i in range(HIST)]
    alpha = [None] * HIST
    for i in reversed(range(HIST)):
        inner = sg[i]
        for j in range(i + 1, HIST):
            inner = inner - alpha[j] * value[ROW_SY[i, j]]
        alpha[i] = rho[i] * inner
    gamma = value[ROW_SY[HIST - 1, HIST - 1]] / value[ROW_YY[HIST - 1, HIST - 1]]
    weight = [None] * HIST
    for i in range(HIST):
        inner = yg[i]
        for j in range(HIST):
            inner = inner - alpha[j] * value[ROW_YY[min(i, j), max(i, j)]]
        inner = gamma * inner
        for j in range(i):
            inner = inner + weight[j] * value[ROW_SY[j, i]]
        weight[i] = alpha[i] - rho[i] * inner

    def finish_rows(n, carry):
        plane = n // (W // 8)
        rows = pl.ds(pl.multiple_of(lax.rem(n, W // 8) * 8, 8), 8)
        g = og_ref[plane, rows] * scale
        og_ref[plane, rows] = g
        nd_ref[plane, rows] = g - last_v[plane, rows]
        q = g
        for i in range(HIST):
            q = q - alpha[i] * y_v[i, plane, rows]
        q = gamma * q
        for i in range(HIST):
            q = q + weight[i] * s_v[i, plane, rows]
        dir_ref[plane, rows] = -q
        return carry

    lax.fori_loop(0, flat // 8, finish_rows, 0, unroll=8)

    weight_live = per_live[0:1]
    for d in range(n_col):
        col = lax.rem(b + n_col - d, n_col) * part
        found = mix2 if d == 0 else col_in.at[d - 1]
        for half in range(2):
            parts = [found[1 + half * part + n] * weight_live for n in range(part)]
            pg_ref[plane_rows(core if half == 0 else 1 - core, col, part)] = jnp.concatenate(parts, 0)
    drain(col_in, sum_send.at[3])


def store(a, b, c, d, a_out, b_out, c_out, d_out, sem):
    copies = [
        pltpu.make_async_copy(src, dst, sem.at[n])
        for n, (src, dst) in enumerate(((a, a_out), (b, b_out), (c, c_out), (d, d_out)))
    ]
    for copy in copies:
        copy.start()
    for copy in copies:
        copy.wait()


def body(n_row, n_col, object_tiles, probe, amplitudes, offsets, counts, past_steps, past_diffs, last_gradient):
    slots = amplitudes.shape[0]
    part = W // n_col
    object_tiles, probe, amplitudes, offsets, past_steps, past_diffs, last_gradient, tables = [
        pltpu.with_memory_space_constraint(x, pltpu.HBM)
        for x in (
            object_tiles,
            probe,
            amplitudes,
            offsets.T,
            past_steps,
            past_diffs,
            last_gradient,
            jnp.asarray(dft_tables()),
        )
    ]
    plane_pair = jax.ShapeDtypeStruct((2, W, W), F32)
    any_spec = pl.BlockSpec(memory_space=pltpu.HBM)
    vmem_spec = pl.BlockSpec(memory_space=pltpu.VMEM)
    dma = pltpu.SemaphoreType.DMA
    scratch = [
        pltpu.VMEM((4, 4 * H, W), F32),
        pltpu.VMEM((4, 4 * H, W), F32),
        pltpu.VMEM((2, W, W), F32),
        pltpu.VMEM((slots, W, W), F32),
        pltpu.VMEM((HIST, 2, W, W), F32),
        pltpu.VMEM((HIST, 2, W, W), F32),
        pltpu.VMEM((2, W, W), F32),
        pltpu.VMEM((2, W, W), F32),
        pltpu.VMEM((4, 2 * W, 2 * W), BF16),
        pltpu.VMEM((GROUP, 2, W, W), F32),
        pltpu.VMEM((2 * W, GROUP * W), BF16),
        pltpu.VMEM((2 * W, GROUP * W), BF16),
        pltpu.VMEM((GROUP * W, 2 * W), BF16),
        pltpu.VMEM((GROUP * W, 2 * W), BF16),
        pltpu.VMEM((GROUP, 2, 3 * W, W), F32),
        pltpu.VMEM((2 * W, W), F32),
        pltpu.VMEM((2, 2, H, W), F32),
        pltpu.VMEM((2, 2, H, W), F32),
        pltpu.VMEM((4, H, W), F32),
        pltpu.VMEM((4, H, W), F32),
        pltpu.VMEM((4, 2, H, W), F32),
        pltpu.VMEM((4, H, W), F32),
        pltpu.VMEM((W, W), F32),
        pltpu.VMEM((W, W), F32),
        pltpu.VMEM((n_col - 1, part, W), F32),
        pltpu.VMEM((8, W), F32),
        pltpu.VMEM((1 + part, 1, W), F32),
        pltpu.VMEM((n_row - 1, 1 + part, 1, W), F32),
        pltpu.VMEM((1 + 2 * part, 1, W), F32),
        pltpu.VMEM((n_col - 1, 1 + 2 * part, 1, W), F32),
        pltpu.SMEM((2, slots), jnp.int32),
        dma((8,)),
        dma((4,)),
        dma((4,)),
        dma((2,)),
        dma((2,)),
        dma((4,)),
        dma((4,)),
        pltpu.SemaphoreType.REGULAR((3,)),
    ]
    og, direction, pg, nd = pl.pallas_call(
        functools.partial(kernel, n_row, n_col, slots),
        name="ptycho",
        out_shape=(plane_pair, plane_pair, jax.ShapeDtypeStruct((2 * W, W), F32), plane_pair),
        in_specs=[any_spec] * 4 + [pl.BlockSpec(memory_space=pltpu.SMEM)] + [any_spec] * 4,
        out_specs=(vmem_spec,) * 4,
        scratch_shapes=scratch,
        compiler_params=pltpu.CompilerParams(
            collective_id=0, has_side_effects=True, vmem_limit_bytes=40 * 2**20
        ),
    )(
        object_tiles,
        probe,
        amplitudes,
        offsets,
        counts,
        past_steps,
        past_diffs,
        last_gradient,
        tables,
    )
    return pl.pallas_call(
        store,
        name="store",
        out_shape=(plane_pair,) * 4,
        in_specs=[vmem_spec] * 4,
        out_specs=(any_spec,) * 4,
        scratch_shapes=[dma((4,))],
        compiler_params=pltpu.CompilerParams(vmem_limit_bytes=2**20),
    )(og, direction, pg.reshape(2, W, W), nd)


def solution(mesh):
    return jax.shard_map(
        functools.partial(body, mesh.shape["row"], mesh.shape["col"]),
        mesh=mesh,
        in_specs=(
            P(None, "row", "col"),
            P(),
            P(("row", "col"), None, None),
            P(("row", "col"), None),
            P("row", "col"),
            P(None, None, "row", "col"),
            P(None, None, "row", "col"),
            P(None, "row", "col"),
        ),
        out_specs=(P(None, "row", "col"), P(None, "row", "col"), P(), P(None, "row", "col")),
        check_vma=False,
    )
```

```python
import functools
import math

import jax
import jax.numpy as jnp
import numpy as np
from jax import lax
from jax.experimental import pallas as pl
from jax.experimental.pallas import tpu as pltpu
from jax.sharding import PartitionSpec as P

MESH = pl.DeviceIdType.MESH
F32 = jnp.float32
BF16 = jnp.bfloat16
W = 128
H = W // 2
SOFTEN = 0.25
GROUP = 16
HIST = 4

NORTH, SOUTH, WEST, EAST = (-1, 0), (1, 0), (0, -1), (0, 1)
NW, NE, SW, SE = (-1, -1), (-1, 1), (1, -1), (1, 1)
AROUND = (NORTH, SOUTH, WEST, EAST, NW, NE, SW, SE)
SIDES = AROUND[:4]
CORNERS = AROUND[4:]

PAIRS_SY = [(i, j) for i in range(HIST) for j in range(i, HIST)]
PAIRS_YY = [(i, j) for i in range(HIST) for j in range(i, HIST)]
ROW_SY = {pair: n for n, pair in enumerate(PAIRS_SY)}
ROW_YY = {pair: len(PAIRS_SY) + n for n, pair in enumerate(PAIRS_YY)}
ROW_COUNT = len(PAIRS_SY) + len(PAIRS_YY)
ROW_SG = ROW_COUNT + 1
ROW_YG = ROW_SG + HIST
N_DOTS = ROW_YG + HIST


def dft_tables():
    index = np.arange(W)
    angle = (index[:, None] * index[None, :] % W) * (2.0 * math.pi / W)
    cosine = np.cos(angle) / math.sqrt(W)
    sine = np.sin(angle) / math.sqrt(W)
    return np.stack([cosine, sine]).astype(np.float32)


def farthest_first(count):
    return sorted(range(1, count), key=lambda d: -min(d, count - d))


def split(x):
    high = x.astype(BF16)
    return high, (x - high.astype(F32)).astype(BF16)


def mm(a, b):
    return jnp.dot(a, b, preferred_element_type=F32)


def kernel(
    n_row,
    n_col,
    slots,
    obj,
    probe,
    amp,
    off_hbm,
    cnt,
    steps,
    diffs,
    last,
    tabs,
    og_ref,
    dir_ref,
    pg_ref,
    nd_ref,
    pad,
    grad,
    pr_v,
    amp_v,
    s_v,
    y_v,
    last_v,
    trig,
    tab,
    patches,
    xh,
    xl,
    ah,
    al,
    zed,
    pacc,
    side_out,
    side_in,
    corner_out,
    corner_in,
    gside_in,
    gcorner_in,
    dots,
    half_in,
    rs_in,
    grams,
    mix,
    row_in,
    mix2,
    col_in,
    off,
    loc_sem,
    halo_send,
    halo_recv,
    ghalo_send,
    ghalo_recv,
    sum_send,
    sum_recv,
    reach,
):
    a = lax.axis_index("row")
    b = lax.axis_index("col")

    def at(step):
        return (lax.rem(a + step[0] % n_row, n_row), lax.rem(b + step[1] % n_col, n_col))

    def send(src, dst, send_sem, recv_sem, device):
        pltpu.make_async_remote_copy(
            src_ref=src,
            dst_ref=dst,
            send_sem=send_sem,
            recv_sem=recv_sem,
            device_id=device,
            device_id_type=MESH,
        ).start()

    def zero_at(index, edge):
        return jnp.where(index == edge, F32(0.0), F32(1.0))

    keep = {NORTH: zero_at(a, 0), SOUTH: zero_at(a, n_row - 1), WEST: zero_at(b, 0), EAST: zero_at(b, n_col - 1)}
    for dr, dc in CORNERS:
        keep[dr, dc] = keep[dr, 0] * keep[0, dc]

    core = lax.rem(a, 2)
    mate = (a + 1 - 2 * core, b)
    obj_copy = pltpu.make_async_copy(obj, pad.at[0:2, H : H + W], loc_sem.at[0])
    obj_copy.start()
    barrier = pltpu.get_barrier_semaphore()
    for step in CORNERS + SIDES:
        pl.semaphore_signal(barrier, inc=1, device_id=at(step), device_id_type=MESH)
    local = []
    for n, (src, dst) in enumerate(
        ((steps, s_v), (diffs, y_v), (tabs, trig), (probe, pr_v), (amp, amp_v), (last, last_v), (off_hbm, off))
    ):
        copy = pltpu.make_async_copy(src, dst, loc_sem.at[n + 1])
        copy.start()
        local.append(copy)

    def drain(ref, sem):
        pltpu.make_async_copy(ref, ref, sem).wait()

    lane = lax.broadcasted_iota(jnp.int32, (H, W), 1)
    low = lane < H

    def turn(x):
        return pltpu.roll(x, H, 1)

    def pack(first, second):
        return jnp.where(low, first, second)

    obj_copy.wait()
    top = [pad[p, H : 2 * H] for p in range(2)]
    bottom = [pad[p, 2 * H : 3 * H] for p in range(2)]
    for p in range(2):
        side_out[0, p] = pack(top[p], turn(bottom[p]))
        side_out[1, p] = pack(turn(top[p]), bottom[p])
    for n, (dr, dc) in enumerate(CORNERS):
        rows = top if dr < 0 else bottom
        if dc < 0:
            corner_out[n] = pack(rows[0], turn(rows[1]))
        else:
            corner_out[n] = pack(turn(rows[0]), rows[1])

    pl.semaphore_wait(barrier, len(AROUND))

    def tell(n):
        for step in SIDES:
            device = at((step[0] * 2**n, step[1] * 2**n))
            pl.semaphore_signal(reach.at[n], inc=1, device_id=device, device_id_type=MESH)

    def hear(n):
        pl.semaphore_wait(reach.at[n], len(SIDES))


    for n, step in enumerate(CORNERS):
        send(corner_out.at[n], corner_in.at[n], halo_send.at[1], halo_recv.at[1], at(step))
    for n, step in enumerate((WEST, EAST)):
        send(side_out.at[n], side_in.at[n], halo_send.at[0], halo_recv.at[0], at(step))
    first_rows, last_rows = pad.at[0:2, 0:H], pad.at[0:2, 3 * H : 4 * H]
    send(pad.at[0:2, H : 2 * H], last_rows, halo_send.at[2], halo_recv.at[2], at(NORTH))
    send(pad.at[0:2, 2 * H : 3 * H], first_rows, halo_send.at[3], halo_recv.at[3], at(SOUTH))

    tell(0)

    for copy in local[:2]:
        copy.wait()
    dots[...] = jnp.zeros_like(dots)
    flat = 2 * W

    def gram(n, sums):
        plane = n // (W // 8)
        rows = pl.ds(pl.multiple_of(lax.rem(n, W // 8) * 8, 8), 8)
        s = [s_v[i, plane, rows] for i in range(HIST)]
        y = [y_v[i, plane, rows] for i in range(HIST)]
        products = [s[i] * y[j] for i, j in PAIRS_SY] + [y[i] * y[j] for i, j in PAIRS_YY]
        return tuple(total + one for total, one in zip(sums, products))

    sums = lax.fori_loop(0, flat // 8, gram, (jnp.zeros((8, W), F32),) * ROW_COUNT, unroll=2)
    for n in range(ROW_COUNT):
        dots[n : n + 1] = jnp.sum(sums[n], 0, keepdims=True)
    local[6].wait()
    live_count = cnt[0, 0]
    lane_row = lax.broadcasted_iota(jnp.int32, (1, W), 1)
    dots[ROW_COUNT : ROW_COUNT + 1] = jnp.where(lane_row == 0, live_count, 0).astype(F32)
    grams[...] = lax.dot_general(
        jnp.ones((8, W), F32),
        dots[...],
        (((1,), (1,)), ((), ())),
        precision=lax.Precision.HIGHEST,
        preferred_element_type=F32,
    )

    hear(0)
    tell(1)
    local[2].wait()
    parts = [split(trig[n]) for n in range(2)]
    for n in range(2):
        cosine, sine = parts[0][n], parts[1][n]
        for base, above, below in ((0, sine, -sine), (2, -sine, sine)):
            tab[base + n, 0:W, 0:W] = cosine
            tab[base + n, W:, W:] = cosine
            tab[base + n, 0:W, W:] = above
            tab[base + n, W:, 0:W] = below

    grad[...] = jnp.zeros_like(grad)
    pacc[...] = jnp.zeros_like(pacc)
    zed[...] = jnp.zeros_like(zed)

    hear(1)
    tell(2)
    for copy in local[3:5]:
        copy.wait()
    for sems in (halo_send, halo_recv):
        for n, ref in enumerate((side_in, corner_in, last_rows, first_rows)):
            drain(ref, sems.at[n])

    for p in range(2):
        pad[p, 0:H] = pad[p, 0:H] * keep[NORTH]
        pad[p, 3 * H : 4 * H] = pad[p, 3 * H : 4 * H] * keep[SOUTH]
        east = side_in[0, p] * keep[EAST]
        west = side_in[1, p] * keep[WEST]
        pad[2 + p, H : 2 * H] = pack(east, turn(west))
        pad[2 + p, 2 * H : 3 * H] = pack(turn(east), west)
    for rows, side in ((slice(0, H), -1), (slice(3 * H, 4 * H), 1)):
        from_east = corner_in[CORNERS.index((-side, -1))] * keep[side, 1]
        from_west = corner_in[CORNERS.index((-side, 1))] * keep[side, -1]
        pad[2, rows] = pack(from_east, turn(from_west))
        pad[3, rows] = pack(turn(from_east), from_west)

    lanes = lax.broadcasted_iota(jnp.int32, (W, W), 1)

    def own(q, iota):
        return (iota >= jnp.maximum(q, 0)) & (iota < jnp.minimum(q + W, W))

    def group(g, carry):
        first = g * GROUP
        offs = []
        for j in range(GROUP):
            k = first + j
            r, c = off[0, k], off[1, k]
            offs.append((r, c))
            inside = own(c - H, lanes)
            part = []
            for p in range(2):
                here = pad[p, pl.ds(r, W)]
                beside = pad[2 + p, pl.ds(r, W)]
                part.append(pltpu.roll(jnp.where(inside, here, beside), lax.rem(W + H - c, W), 1))
                patches[j, p] = part[p]
            pr, pi = pr_v[0], pr_v[1]
            cols = slice(j * W, (j + 1) * W)
            xh[0:W, cols], xl[0:W, cols] = split(pr * part[0] - pi * part[1])
            xh[W : 2 * W, cols], xl[W : 2 * W, cols] = split(pr * part[1] + pi * part[0])

        def left(high, low_part, emit):
            for h in range(GROUP // 2):
                cols = slice(h * 2 * W, (h + 1) * 2 * W)
                out = mm(high, xh[:, cols]) + mm(low_part, xh[:, cols]) + mm(high, xl[:, cols])
                for i in range(2):
                    emit(2 * h + i, out[0:W, i * W : (i + 1) * W], out[W:, i * W : (i + 1) * W])

        def right(high, low_part, emit):
            for h in range(GROUP // 2):
                rows = slice(h * 2 * W, (h + 1) * 2 * W)
                out = mm(ah[rows], high) + mm(ah[rows], low_part) + mm(al[rows], high)
                for i in range(2):
                    emit(2 * h + i, out[i * W : (i + 1) * W, 0:W], out[i * W : (i + 1) * W, W:])

        def to_rows(j, real, imag):
            rows = slice(j * W, (j + 1) * W)
            ah[rows, 0:W], al[rows, 0:W] = split(real)
            ah[rows, W:], al[rows, W:] = split(imag)

        def to_cols(j, real, imag):
            cols = slice(j * W, (j + 1) * W)
            xh[0:W, cols], xl[0:W, cols] = split(real)
            xh[W:, cols], xl[W:, cols] = split(imag)

        def weigh(j, real, imag):
            inverse = lax.rsqrt(real * real + imag * imag + SOFTEN)
            live = jnp.where(first + j < live_count, F32(2.0), F32(0.0))
            factor = live * (1.0 - amp_v[first + j] * inverse)
            to_rows(j, factor * real, factor * imag)

        def finish(j, real, imag):
            r, c = offs[j]
            pr, pi = pr_v[0], pr_v[1]
            shift = lax.rem(c + H, W)
            zed[j, 0, W : 2 * W] = pltpu.roll(pr * real + pi * imag, shift, 1)
            zed[j, 1, W : 2 * W] = pltpu.roll(pr * imag - pi * real, shift, 1)
            o_re, o_im = patches[j, 0], patches[j, 1]
            pacc[0:W] += o_re * real + o_im * imag
            pacc[W:] += o_re * imag - o_im * real

        left(tab[0], tab[1], to_rows)
        right(tab[2], tab[3], weigh)
        right(tab[0], tab[1], to_cols)
        left(tab[2], tab[3], finish)

        inside = [own(c - H, lane_row).astype(F32) for _, c in offs]
        for ch in range(4):
            rows = slice(ch * H, (ch + 1) * H)
            for p in range(2):
                here, beside = grad[p, rows], grad[2 + p, rows]
                for j in range(GROUP):
                    moved = zed[j, p, pl.ds(W - offs[j][0] + ch * H, H)]
                    kept = moved * inside[j]
                    here += kept
                    beside += moved - kept
                grad[p, rows], grad[2 + p, rows] = here, beside
        return carry

    lax.fori_loop(0, slots // GROUP, group, 0)

    other_plane = pl.ds(pl.multiple_of((1 - core) * W, W), W)
    send(pacc.at[other_plane], half_in, sum_send.at[0], sum_recv.at[0], mate)

    for p in range(2):
        upper, lower = grad[2 + p, H : 2 * H], grad[2 + p, 2 * H : 3 * H]
        side_out[0, p] = pack(turn(upper), lower)
        side_out[1, p] = pack(upper, turn(lower))
    for n, (dr, dc) in enumerate(CORNERS):
        rows = slice(0, H) if dr < 0 else slice(3 * H, 4 * H)
        first, second = grad[2, rows], grad[3, rows]
        corner_out[n] = pack(turn(first), second) if dc < 0 else pack(first, turn(second))
    for n, step in enumerate(CORNERS):
        send(corner_out.at[n], gcorner_in.at[n], ghalo_send.at[1], ghalo_recv.at[1], at(step))
    for n, (src, step) in enumerate(
        (
            (side_out.at[0], WEST),
            (side_out.at[1], EAST),
            (grad.at[0:2, 0:H], NORTH),
            (grad.at[0:2, 3 * H : 4 * H], SOUTH),
        )
    ):
        send(src, gside_in.at[n], ghalo_send.at[0], ghalo_recv.at[0], at(step))

    part = W // n_col

    def plane_rows(plane, start, size):
        return pl.ds(pl.multiple_of(plane * W + start, 8), size)

    hear(2)
    drain(half_in, sum_recv.at[0])
    pacc[plane_rows(core, 0, W)] += half_in[...]
    for d in farthest_first(n_col):
        rows = plane_rows(core, lax.rem(b + d, n_col) * part, part)
        send(pacc.at[rows], rs_in.at[d - 1], sum_send.at[1], sum_recv.at[1], at((0, d)))

    drain(gside_in, ghalo_recv.at[0])
    drain(gcorner_in, ghalo_recv.at[1])
    for p in range(2):
        east, west = gside_in[0, p] * keep[EAST], gside_in[1, p] * keep[WEST]
        for side, mid in ((-1, pack(west, turn(east))), (1, pack(turn(west), east))):
            from_east = gcorner_in[CORNERS.index((-side, -1))] * keep[side, 1]
            from_west = gcorner_in[CORNERS.index((-side, 1))] * keep[side, -1]
            if p == 0:
                corner = pack(from_west, turn(from_east))
            else:
                corner = pack(turn(from_west), from_east)
            vertical = gside_in[3 if side < 0 else 2, p] * keep[side, 0]
            mine = grad[p, H : 2 * H] if side < 0 else grad[p, 2 * H : 3 * H]
            if side < 0:
                og_ref[p, 0:H] = mine + vertical + mid + corner
            else:
                og_ref[p, H:] = mine + vertical + mid + corner

    def with_gradient(n, sums):
        plane = n // (W // 8)
        rows = pl.ds(pl.multiple_of(lax.rem(n, W // 8) * 8, 8), 8)
        g = og_ref[plane, rows]
        products = [s_v[i, plane, rows] * g for i in range(HIST)] + [y_v[i, plane, rows] * g for i in range(HIST)]
        return tuple(total + one for total, one in zip(sums, products))

    sums = lax.fori_loop(
        0, flat // 8, with_gradient, (jnp.zeros((8, W), F32),) * (2 * HIST), unroll=8
    )
    row8 = lax.broadcasted_iota(jnp.int32, (8, W), 0)
    lane8 = lax.broadcasted_iota(jnp.int32, (8, W), 1)
    inner = jnp.zeros((8, W), F32)
    for n in range(2 * HIST):
        inner = jnp.where(row8 == n, jnp.sum(sums[n], 0, keepdims=True), inner)
    inner = jnp.sum(inner, 1, keepdims=True)
    inner = jnp.where(lane8 == ROW_SG + row8, inner, jnp.where(row8 == 0, grams[...], 0.0))
    mix[0] = jnp.sum(inner, 0, keepdims=True)

    drain(rs_in, sum_recv.at[1])
    total = pacc[plane_rows(core, b * part, part)]
    for d in range(n_col - 1):
        total += rs_in[d]
    for n in range(part):
        mix[1 + n] = total[n : n + 1]

    for d in farthest_first(n_row):
        send(mix, row_in.at[d - 1], sum_send.at[2], sum_recv.at[2], at((d, 0)))
    drain(half_in, sum_send.at[0])
    drain(rs_in, sum_send.at[1])
    drain(gside_in, ghalo_send.at[0])
    drain(gcorner_in, ghalo_send.at[1])
    drain(row_in, sum_recv.at[2])
    own, odd = mix[...], row_in[0]
    for d in range(2, n_row):
        if d % 2 == 0:
            own += row_in[d - 1]
        else:
            odd += row_in[d - 1]
    mix2[0] = own[0] + odd[0]
    mix2[1 : 1 + part] = own[1:]
    mix2[1 + part :] = odd[1:]

    for d in farthest_first(n_col):
        send(mix2, col_in.at[d - 1], sum_send.at[3], sum_recv.at[3], at((0, d)))
    drain(row_in, sum_send.at[2])
    local[5].wait()
    drain(col_in, sum_recv.at[3])
    total = mix2[0]
    for d in range(n_col - 1):
        total += col_in[d, 0]
    total = jnp.broadcast_to(total, (8, W))

    value = [jnp.broadcast_to(total[:, n : n + 1], (8, W)) for n in range(N_DOTS)]
    live_total = value[ROW_COUNT]
    per_live = 1.0 / live_total
    scale = (n_row * n_col) * per_live
    sg = [value[ROW_SG + i] * scale for i in range(HIST)]
    yg = [value[ROW_YG + i] * scale for i in range(HIST)]
    rho = [1.0 / value[ROW_SY[i, i]] for i in range(HIST)]
    alpha = [None] * HIST
    for i in reversed(range(HIST)):
        inner = sg[i]
        for j in range(i + 1, HIST):
            inner = inner - alpha[j] * value[ROW_SY[i, j]]
        alpha[i] = rho[i] * inner
    gamma = value[ROW_SY[HIST - 1, HIST - 1]] / value[ROW_YY[HIST - 1, HIST - 1]]
    weight = [None] * HIST
    for i in range(HIST):
        inner = yg[i]
        for j in range(HIST):
            inner = inner - alpha[j] * value[ROW_YY[min(i, j), max(i, j)]]
        inner = gamma * inner
        for j in range(i):
            inner = inner + weight[j] * value[ROW_SY[j, i]]
        weight[i] = alpha[i] - rho[i] * inner

    def finish_rows(n, carry):
        plane = n // (W // 8)
        rows = pl.ds(pl.multiple_of(lax.rem(n, W // 8) * 8, 8), 8)
        g = og_ref[plane, rows] * scale
        og_ref[plane, rows] = g
        nd_ref[plane, rows] = g - last_v[plane, rows]
        q = g
        for i in range(HIST):
            q = q - alpha[i] * y_v[i, plane, rows]
        q = gamma * q
        for i in range(HIST):
            q = q + weight[i] * s_v[i, plane, rows]
        dir_ref[plane, rows] = -q
        return carry

    lax.fori_loop(0, flat // 8, finish_rows, 0, unroll=8)

    weight_live = per_live[0:1]
    for d in range(n_col):
        col = lax.rem(b + n_col - d, n_col) * part
        found = mix2 if d == 0 else col_in.at[d - 1]
        for half in range(2):
            parts = [found[1 + half * part + n] * weight_live for n in range(part)]
            pg_ref[plane_rows(core if half == 0 else 1 - core, col, part)] = jnp.concatenate(parts, 0)
    drain(col_in, sum_send.at[3])


def store(a, b, c, d, a_out, b_out, c_out, d_out, sem):
    copies = [
        pltpu.make_async_copy(src, dst, sem.at[n])
        for n, (src, dst) in enumerate(((a, a_out), (b, b_out), (c, c_out), (d, d_out)))
    ]
    for copy in copies:
        copy.start()
    for copy in copies:
        copy.wait()


def body(n_row, n_col, object_tiles, probe, amplitudes, offsets, counts, past_steps, past_diffs, last_gradient):
    slots = amplitudes.shape[0]
    part = W // n_col
    object_tiles, probe, amplitudes, offsets, past_steps, past_diffs, last_gradient, tables = [
        pltpu.with_memory_space_constraint(x, pltpu.HBM)
        for x in (
            object_tiles,
            probe,
            amplitudes,
            offsets.T,
            past_steps,
            past_diffs,
            last_gradient,
            jnp.asarray(dft_tables()),
        )
    ]
    plane_pair = jax.ShapeDtypeStruct((2, W, W), F32)
    any_spec = pl.BlockSpec(memory_space=pltpu.HBM)
    vmem_spec = pl.BlockSpec(memory_space=pltpu.VMEM)
    dma = pltpu.SemaphoreType.DMA
    scratch = [
        pltpu.VMEM((4, 4 * H, W), F32),
        pltpu.VMEM((4, 4 * H, W), F32),
        pltpu.VMEM((2, W, W), F32),
        pltpu.VMEM((slots, W, W), F32),
        pltpu.VMEM((HIST, 2, W, W), F32),
        pltpu.VMEM((HIST, 2, W, W), F32),
        pltpu.VMEM((2, W, W), F32),
        pltpu.VMEM((2, W, W), F32),
        pltpu.VMEM((4, 2 * W, 2 * W), BF16),
        pltpu.VMEM((GROUP, 2, W, W), F32),
        pltpu.VMEM((2 * W, GROUP * W), BF16),
        pltpu.VMEM((2 * W, GROUP * W), BF16),
        pltpu.VMEM((GROUP * W, 2 * W), BF16),
        pltpu.VMEM((GROUP * W, 2 * W), BF16),
        pltpu.VMEM((GROUP, 2, 3 * W, W), F32),
        pltpu.VMEM((2 * W, W), F32),
        pltpu.VMEM((2, 2, H, W), F32),
        pltpu.VMEM((2, 2, H, W), F32),
        pltpu.VMEM((4, H, W), F32),
        pltpu.VMEM((4, H, W), F32),
        pltpu.VMEM((4, 2, H, W), F32),
        pltpu.VMEM((4, H, W), F32),
        pltpu.VMEM((W, W), F32),
        pltpu.VMEM((W, W), F32),
        pltpu.VMEM((n_col - 1, part, W), F32),
        pltpu.VMEM((8, W), F32),
        pltpu.VMEM((1 + part, 1, W), F32),
        pltpu.VMEM((n_row - 1, 1 + part, 1, W), F32),
        pltpu.VMEM((1 + 2 * part, 1, W), F32),
        pltpu.VMEM((n_col - 1, 1 + 2 * part, 1, W), F32),
        pltpu.SMEM((2, slots), jnp.int32),
        dma((8,)),
        dma((4,)),
        dma((4,)),
        dma((2,)),
        dma((2,)),
        dma((4,)),
        dma((4,)),
        pltpu.SemaphoreType.REGULAR((3,)),
    ]
    og, direction, pg, nd = pl.pallas_call(
        functools.partial(kernel, n_row, n_col, slots),
        name="ptycho",
        out_shape=(plane_pair, plane_pair, jax.ShapeDtypeStruct((2 * W, W), F32), plane_pair),
        in_specs=[any_spec] * 4 + [pl.BlockSpec(memory_space=pltpu.SMEM)] + [any_spec] * 4,
        out_specs=(vmem_spec,) * 4,
        scratch_shapes=scratch,
        compiler_params=pltpu.CompilerParams(
            collective_id=0, has_side_effects=True, vmem_limit_bytes=40 * 2**20
        ),
    )(
        object_tiles,
        probe,
        amplitudes,
        offsets,
        counts,
        past_steps,
        past_diffs,
        last_gradient,
        tables,
    )
    return pl.pallas_call(
        store,
        name="store",
        out_shape=(plane_pair,) * 4,
        in_specs=[vmem_spec] * 4,
        out_specs=(any_spec,) * 4,
        scratch_shapes=[dma((4,))],
        compiler_params=pltpu.CompilerParams(vmem_limit_bytes=2**20),
    )(og, direction, pg.reshape(2, W, W), nd)


def solution(mesh):
    return jax.shard_map(
        functools.partial(body, mesh.shape["row"], mesh.shape["col"]),
        mesh=mesh,
        in_specs=(
            P(None, "row", "col"),
            P(),
            P(("row", "col"), None, None),
            P(("row", "col"), None),
            P("row", "col"),
            P(None, None, "row", "col"),
            P(None, None, "row", "col"),
            P(None, "row", "col"),
        ),
        out_specs=(P(None, "row", "col"), P(None, "row", "col"), P(), P(None, "row", "col")),
        check_vma=False,
    )
```
